32 devices in a mesh: date: 4 (over y, x), space: 8 (over z, core).
Axes of the slice: x: 2, y: 2, z: 4, core: 2. Of those that a mesh axis runs over, the one named last changes fastest.
Arguments:
- acquisitions: bfloat16 [2, 128, 192, 576], P(None, 'date', 'space'), may hold values from -6 to 6
- valid_dates: int32 [128, 192, 576], P('date', 'space'), may hold values 0 or 1
Outputs:
- linked: float32 [2, 128, 32, 192], P(None, 'date', 'space')
The draws below stay inside these ranges and needn't reach their ends.
All inputs are finite; a program needn't handle non-finite values. No bound on the sum of `valid_dates` on one device may be relied on, other than what follows from the above.
Results may differ from the reference program's by a relative error of at most 0.0028.
Values may be sent and summed in bfloat16 or wider, within the bound.
No kernel may reach another device: no remote copies, remote signals or barrier semaphores. Data moves between devices by JAX's collectives and lax.ppermute only.
A program may use at most 256 MiB of HBM per device.

```python
import jax
import jax.numpy as jnp
from jax import lax

DATES = 128
BOX_ROWS = 15
BOX_COLS = 7
STEP_ROWS = 3
STEP_COLS = 6
ITERS = 4
MARGIN = 6
NBOX = 105
ROWS = 576
COLS = 192
OUTROWS = 192


def set_ends(drawn, key, low, high):
    longest = drawn.shape.index(max(drawn.shape))
    spots = []
    for shift in (0, 1):
        where = [jax.random.randint(jax.random.fold_in(key, axis), (), 0, length) for axis, length in enumerate(drawn.shape)]
        where[longest] = (where[longest] + shift) % drawn.shape[longest]
        spots.append(tuple(where))
    return drawn.at[spots[0]].set(low).at[spots[1]].set(high)


def levels(stream_key, dims, shards, smallest, largest):
    factor_of = 1.0
    for position, shards_of in shards:
        steps = jax.random.uniform(jax.random.fold_in(jax.random.fold_in(stream_key, 6), position), (shards_of,), jnp.float32, smallest / len(shards), largest / len(shards))
        factor_of = factor_of * jnp.repeat(jnp.exp(steps), dims[position] // shards_of).reshape((-1,) + (1,) * (len(dims) - 1 - position))
    return factor_of


def centred(stream_key, shape, spread, bound, split=(), kind=jnp.bfloat16):
    values = jax.random.normal(stream_key, shape, jnp.float32) * spread
    if len(split) > 0:
        values = levels(stream_key, shape, split, -0.22, 0.18) * values
    return jnp.clip(values, min=-bound, max=bound).astype(kind)


def setup_inputs(seed: int = 0) -> dict:
    key_list = jax.random.split(jax.random.key(seed), 3)
    return {
        "acquisitions": centred(key_list[0], (2, DATES, COLS, ROWS), 1.0, 6.0, ((1, 4), (2, 8))),
        "valid_dates": set_ends((jax.random.randint(key_list[1], (DATES, COLS, ROWS), 0, 4) < 3).astype(jnp.int32), jax.random.fold_in(key_list[1], 1), 0, 1),
    }


POWER_EPS = 1e-05

def reference(acquisitions, valid_dates):
    masked = acquisitions * valid_dates.astype(jnp.bfloat16)[None]
    masked = jnp.swapaxes(masked, 2, 3)
    left_pad = STEP_COLS // 2
    framed = jnp.pad(masked, ((0, 0), (0, 0), (MARGIN, MARGIN), (left_pad, BOX_COLS - STEP_COLS)))
    out_cols = COLS // STEP_COLS
    span = STEP_COLS * (out_cols - 1) + 1

    def link_row(out_row):
        band_rows = lax.dynamic_slice_in_dim(framed, out_row * STEP_ROWS, BOX_ROWS, 2)
        window = jnp.stack([band_rows[..., k:k + span:STEP_COLS] for k in range(BOX_COLS)], axis=3)
        window = window.astype(jnp.float32)
        real_sum = jnp.einsum('adrkc,aerkc->cde', window, window, precision=lax.Precision.HIGHEST)
        cross_sum = jnp.einsum('drkc,erkc->cde', window[1], window[0], precision=lax.Precision.HIGHEST)
        energy = jnp.diagonal(real_sum, axis1=1, axis2=2) / NBOX + POWER_EPS
        factor = lax.rsqrt(energy)
        weights = factor[:, :, None] * factor[:, None, :] / NBOX
        coh_real = (real_sum * weights).astype(jnp.bfloat16).astype(jnp.float32)
        coh_imag = ((cross_sum - jnp.swapaxes(cross_sum, 1, 2)) * weights).astype(jnp.bfloat16).astype(jnp.float32)
        vec_real = jnp.ones((out_cols, DATES), jnp.float32)
        vec_imag = jnp.zeros((out_cols, DATES), jnp.float32)
        for sweep in range(ITERS):
            real_out = jnp.einsum('cde,ce->cd', coh_real, vec_real, precision=lax.Precision.HIGHEST) - jnp.einsum('cde,ce->cd', coh_imag, vec_imag, precision=lax.Precision.HIGHEST)
            imag_out = jnp.einsum('cde,ce->cd', coh_imag, vec_real, precision=lax.Precision.HIGHEST) + jnp.einsum('cde,ce->cd', coh_real, vec_imag, precision=lax.Precision.HIGHEST)
            total = lax.optimization_barrier(jnp.sum(real_out * real_out + imag_out * imag_out, axis=1)) / DATES + POWER_EPS
            norm_factor = lax.rsqrt(total)[:, None]
            vec_real = real_out * norm_factor
            vec_imag = imag_out * norm_factor
            if sweep + 1 < ITERS:
                vec_real = vec_real.astype(jnp.bfloat16).astype(jnp.float32)
                vec_imag = vec_imag.astype(jnp.bfloat16).astype(jnp.float32)
        return jnp.stack([vec_real, vec_imag])
    rows_out = lax.map(link_row, jnp.arange(OUTROWS, dtype=jnp.int32))
    return jnp.transpose(rows_out, (1, 3, 2, 0))
```

```python
import functools
import math

import jax
import jax.numpy as jnp
from jax import lax
from jax.experimental import pallas as pl
from jax.experimental.pallas import tpu as pltpu
from jax.sharding import PartitionSpec as P

BOX_ROWS = 15
BOX_COLS = 7
STEP_ROWS = 3
STEP_COLS = 6
ITERS = 4
MARGIN = 6
NBOX = 105
POWER_EPS = 1e-05

LANES = 128
TILE_ROWS = 18
SLOTS = TILE_ROWS // STEP_ROWS
LEAD = MARGIN // STEP_ROWS
LEFT = STEP_COLS // 2
BATCH = 24
CONTRACT_LAST = (((1,), (1,)), ((), ()))


def lane_mask(shape, first, count):
    lane = lax.broadcasted_iota(jnp.int32, shape, len(shape) - 1)
    inside = ((lane - first) & (LANES - 1)) < count
    return jnp.where(inside, 1.0, 0.0).astype(jnp.bfloat16)


def pack_kernel(tiles, col_groups, segments, axis, acq_ref, valid_ref, halo_ref, *refs):
    outs, planes = refs[:-1], refs[-1]
    parts, dates, cols, rows = acq_ref.shape
    blocks = planes.shape[1]
    stride = planes.shape[2] // dates
    me = lax.axis_index(axis)
    for part in range(parts):
        for block in range(blocks):
            width = min(LANES, rows - block * LANES)
            span = slice(block * LANES, block * LANES + width)
            if width < LANES:
                planes[part, block] = jnp.zeros(planes.shape[2:], jnp.float32)
            for date in range(dates):
                value = acq_ref[part, date, :, span].astype(jnp.float32) * valid_ref[
                    date, :, span
                ].astype(jnp.float32)
                planes[part, block, date * stride : date * stride + cols, :width] = value
                planes[
                    part, block, date * stride + cols : date * stride + cols + LEFT, :width
                ] = halo_ref[part, date, :, span].astype(jnp.float32)
    for offset, out in enumerate(outs):
        target = me ^ offset
        group = lax.rem(target, col_groups)
        segment = target // col_groups

        def source(part, block, j):
            column = group * STEP_COLS - LEFT + j
            column = jnp.where(column < 0, column + cols + LEFT, column)
            plane = planes[part, block, pl.ds(column, dates, stride=stride), :]
            if j:
                plane = pltpu.roll(plane, TILE_ROWS * j, 1)
            return plane.astype(jnp.bfloat16)

        if segments == 1:
            held = {}
            for part in range(parts):
                for tile in range(tiles):
                    total = None
                    first_row = tile * TILE_ROWS
                    for j in range(BOX_COLS):
                        row = first_row
                        while row < first_row + TILE_ROWS:
                            block = row // LANES
                            stop = min(first_row + TILE_ROWS, (block + 1) * LANES)
                            if (part, block, j) not in held:
                                held[part, block, j] = source(part, block, j)
                            mask = lane_mask((16, LANES), (row + TILE_ROWS * j) % LANES, stop - row)
                            piece = held[part, block, j].reshape(-1, 16, LANES) * mask[None]
                            total = piece if total is None else total + piece
                            row = stop
                    out[tile, part] = total.reshape(dates, LANES)
        else:

            def one(index, carry):
                tile = segment * tiles + index - 1
                first_row = jnp.clip(tile, 0, segments * tiles - 1) * TILE_ROWS
                kept = jnp.where((tile >= 0) & (tile < segments * tiles), 1.0, 0.0)
                low = first_row // LANES
                high = (first_row + TILE_ROWS - 1) // LANES
                split = jnp.minimum(high * LANES - first_row, TILE_ROWS)
                split = jnp.where(high == low, TILE_ROWS, split)
                for part in range(parts):
                    total = jnp.zeros((dates // 16, 16, LANES), jnp.bfloat16)
                    for j in range(BOX_COLS):
                        start = first_row + TILE_ROWS * j
                        for block, first, count in (
                            (low, start, split),
                            (high, start + split, TILE_ROWS - split),
                        ):
                            mask = lane_mask((16, LANES), first & (LANES - 1), count)
                            piece = source(part, block, j).reshape(-1, 16, LANES)
                            total = total + piece * mask[None]
                    total = total * kept.astype(jnp.bfloat16)
                    out[index, part] = total.reshape(dates, LANES)
                return carry

            lax.fori_loop(0, tiles + 2, one, 0)


def pack(acquisitions, valid_dates, halo, axis, peers, tiles, col_groups, segments):
    parts, dates, cols, rows = acquisitions.shape
    sent = tiles if segments == 1 else tiles + 2
    shape = jax.ShapeDtypeStruct((sent, parts, dates, LANES), jnp.bfloat16)
    whole = pl.BlockSpec(memory_space=pltpu.VMEM)
    return pl.pallas_call(
        functools.partial(pack_kernel, tiles, col_groups, segments, axis),
        out_shape=[shape] * peers,
        in_specs=[whole] * 3,
        out_specs=[whole] * peers,
        scratch_shapes=[
            pltpu.VMEM((parts, -(-rows // LANES), dates * 32, LANES), jnp.float32),
        ],
        compiler_params=pltpu.CompilerParams(vmem_limit_bytes=56 << 20),
        name="pack",
    )(acquisitions, valid_dates, halo)


def slot_rows(first):
    lane = lax.broadcasted_iota(jnp.int32, (16, LANES), 1)
    place = (lane - first) & (LANES - 1)
    column = (place * 57) >> 10
    return place - TILE_ROWS * column, column < BOX_COLS


def as_mask(inside):
    return jnp.where(inside, 1.0, 0.0).astype(jnp.bfloat16)[None]


def window_pair(real, imag, k, e, row_now, row_next):
    shape = (-1, 16, LANES)
    if e == 0:
        now = as_mask((row_now >= 0) & (row_now < BOX_ROWS))
    else:
        now = as_mask(row_now >= STEP_ROWS * e)
    a = real[k].reshape(shape) * now
    b = imag[k].reshape(shape) * now
    rest = STEP_ROWS * e + BOX_ROWS - TILE_ROWS
    if rest > 0:
        after = as_mask(row_next < rest)
        a = a + real[k + 1].reshape(shape) * after
        b = b + imag[k + 1].reshape(shape) * after
    return a.reshape(real.shape[1:]), b.reshape(real.shape[1:])


def coherence(a, b, diagonal, held, place):
    count = a.shape[0]
    right = jnp.concatenate([a, b], axis=1)
    left = jnp.concatenate([right, jnp.concatenate([b, -a], axis=1)], axis=0)
    sums = lax.dot_general(left, right, CONTRACT_LAST, preferred_element_type=jnp.float32)
    real, imag = sums[:count], sums[count:]
    energy = jnp.sum(jnp.where(diagonal, real, 0.0), axis=0, keepdims=True) * (1 / NBOX)
    factor = lax.rsqrt(energy + POWER_EPS)
    down = jnp.sum(jnp.where(diagonal, factor, 0.0), axis=1, keepdims=True)
    weights = down * (factor * (1 / NBOX))
    held[place, :count] = (real * weights).astype(jnp.bfloat16)
    held[place, count:] = (imag * weights).astype(jnp.bfloat16)


def iterate(held, pixels, dates):
    row = lax.broadcasted_iota(jnp.int32, (8, dates), 0)
    odd = (row & 1) == 1
    sign = jnp.where((row & 2) == 2, -1.0, 1.0)
    start = jnp.concatenate([jnp.where(odd, 0.0, sign), jnp.where(odd, -sign, 0.0)], axis=1)
    vectors = [start.astype(jnp.bfloat16)] * pixels
    for sweep in range(ITERS):
        scaled = []
        for place in range(pixels):
            product = jnp.dot(vectors[place], held[place], preferred_element_type=jnp.float32)
            square = product * product
            square = square + pltpu.roll(square, 1, 0)
            total = jnp.sum(square, axis=1, keepdims=True) * (1 / dates) + POWER_EPS
            scaled.append(product * lax.rsqrt(total))
        if sweep + 1 < ITERS:
            vectors = [
                jnp.concatenate([v, pltpu.roll(v, 7, 0)], axis=1).astype(jnp.bfloat16)
                for v in scaled
            ]
    return scaled


def link_kernel(peers, padded, *refs):
    sources, outs = refs[:peers], refs[peers : 2 * peers]
    real, imag, held, linked = refs[2 * peers :]
    sent, _, dates, _ = sources[0].shape
    all_dates = peers * dates
    base = 0 if padded else 1
    for peer, source in enumerate(sources):
        span = slice(peer * dates, (peer + 1) * dates)
        real[base : base + sent, span] = source[:, 0]
        imag[base : base + sent, span] = source[:, 1]
    if not padded:
        zero = jnp.zeros((all_dates, LANES), jnp.bfloat16)
        for tiles in (real, imag):
            tiles[0] = zero
            tiles[sent + 1] = zero
    pixels = linked.shape[0] // 8
    batch = math.gcd(BATCH, pixels)
    diagonal = lax.broadcasted_iota(
        jnp.int32, (all_dates, all_dates), 0
    ) == lax.broadcasted_iota(jnp.int32, (all_dates, all_dates), 1)

    def step(index, carry):
        rows_of = {}

        def rows_at(k):
            if k not in rows_of:
                first = (index * (batch // SLOTS) + k - 1) * TILE_ROWS
                if padded:
                    segment = lax.axis_index("date") // padded
                    first = first + segment * (sent - 2) * TILE_ROWS
                row, used = slot_rows(first)
                rows_of[k] = jnp.where(used, row, -1), jnp.where(used, row, LANES)
            return rows_of[k]

        for place in range(batch):
            k, e = divmod(place + SLOTS - LEAD, SLOTS)
            a, b = window_pair(
                real, imag, index * (batch // SLOTS) + k, e, rows_at(k)[0], rows_at(k + 1)[1]
            )
            coherence(a, b, diagonal, held, place)
        for place, tile in enumerate(iterate(held, batch, all_dates)):
            linked[pl.ds((index * batch + place) * 8, 8)] = tile
        return carry

    lax.fori_loop(0, pixels // batch, step, 0)
    for part in range(2):
        vectors = linked[pl.ds(part, pixels, stride=8), :]
        flat = jnp.transpose(vectors)
        for peer, out in enumerate(outs):
            out[part] = flat[peer * dates : (peer + 1) * dates]


def link(sources, pixels, padded):
    peers = len(sources)
    sent, parts, dates, _ = sources[0].shape
    all_dates = peers * dates
    kept = sent if padded else sent + 2
    shape = jax.ShapeDtypeStruct((parts, dates, pixels), jnp.float32)
    whole = pl.BlockSpec(memory_space=pltpu.VMEM)
    return pl.pallas_call(
        functools.partial(link_kernel, peers, padded),
        out_shape=[shape] * peers,
        in_specs=[whole] * peers,
        out_specs=[whole] * peers,
        scratch_shapes=[
            pltpu.VMEM((kept, all_dates, LANES), jnp.bfloat16),
            pltpu.VMEM((kept, all_dates, LANES), jnp.bfloat16),
            pltpu.VMEM((math.gcd(BATCH, pixels), 2 * all_dates, all_dates), jnp.bfloat16),
            pltpu.VMEM((pixels * 8, all_dates), jnp.float32),
        ],
        compiler_params=pltpu.CompilerParams(vmem_limit_bytes=56 << 20),
        name="link",
    )(*sources)


def swap(blocks, axis):
    count = len(blocks)
    return [blocks[0]] + [
        lax.ppermute(blocks[m], axis, [(i, i ^ m) for i in range(count)]) for m in range(1, count)
    ]


def on_device(acquisitions, valid_dates):
    peers = lax.axis_size("date")
    strips = lax.axis_size("space")
    parts, dates, cols, rows = acquisitions.shape
    out_cols = cols // STEP_COLS
    segments = peers // out_cols
    tiles = rows // TILE_ROWS // segments
    pixels = rows // STEP_ROWS // segments
    edge = acquisitions[:, :, cols - LEFT :] * valid_dates[:, cols - LEFT :].astype(jnp.bfloat16)
    halo = lax.ppermute(edge, "space", [(i, i + 1) for i in range(strips - 1)])
    outgoing = pack(acquisitions, valid_dates, halo, "date", peers, tiles, out_cols, segments)
    incoming = swap(outgoing, "date")
    outgoing = link(incoming, pixels, 0 if segments == 1 else out_cols)
    incoming = swap(outgoing, "date")
    me = lax.axis_index("date")
    columns = []
    for target in range(peers):
        block = incoming[target]
        for other in range(1, peers):
            block = jnp.where(me == other, incoming[target ^ other], block)
        columns.append(block)
    strips_out = [
        jnp.concatenate(columns[c::out_cols], axis=2) if segments > 1 else columns[c]
        for c in range(out_cols)
    ]
    return jnp.stack(strips_out, axis=2)


def solution(mesh):
    in_specs = (P(None, "date", "space", None), P("date", "space", None))
    out_specs = P(None, "date", "space", None)
    return jax.shard_map(
        on_device, mesh=mesh, in_specs=in_specs, out_specs=out_specs, check_vma=False
    )
```

```python
import functools
import math

import jax
import jax.numpy as jnp
from jax import lax
from jax.experimental import pallas as pl
from jax.experimental.pallas import tpu as pltpu
from jax.sharding import PartitionSpec as P

BOX_ROWS = 15
BOX_COLS = 7
STEP_ROWS = 3
STEP_COLS = 6
ITERS = 4
MARGIN = 6
NBOX = 105
POWER_EPS = 1e-05

LANES = 128
TILE_ROWS = 18
SLOTS = TILE_ROWS // STEP_ROWS
LEAD = MARGIN // STEP_ROWS
LEFT = STEP_COLS // 2
BATCH = 48
CHUNKS = (4,)
CONTRACT_LAST = (((1,), (1,)), ((), ()))


def lane_mask(first, count):
    lane = lax.broadcasted_iota(jnp.int32, (16, LANES), 1)
    inside = ((lane - first) & (LANES - 1)) < count
    return (jnp.where(inside, 1.0, 0.0).astype(jnp.bfloat16) > 0)[None]


def choose(mask, yes, no):
    return jnp.where(jnp.broadcast_to(mask, yes.shape), yes, no)


def edge_kernel(first, *refs):
    acq_ref, valid_ref, out, planes = refs
    parts, dates, _, rows = acq_ref.shape
    stride = planes.shape[2] // dates
    span = slice(first // 8 * 8, first // 8 * 8 + 8)
    offset = first % 8

    def one_date(date, carry):
        keep = valid_ref[date, span].astype(jnp.float32)
        for part in range(parts):
            value = acq_ref[part, date, span].astype(jnp.float32) * keep
            for block in range(planes.shape[1]):
                width = min(LANES, rows - block * LANES)
                planes[part, block, pl.ds(date * stride, 8), :width] = value[
                    :, block * LANES : block * LANES + width
                ]
        return carry

    for part in range(parts):
        planes[part, planes.shape[1] - 1] = jnp.zeros(planes.shape[2:], jnp.float32)
    lax.fori_loop(0, dates, one_date, 0, unroll=4)
    for j in range(LEFT):
        for part in range(parts):
            for block in range(planes.shape[1]):
                plane = planes[part, block, pl.ds(offset + j, dates, stride=stride), :]
                out[j, part, :, block * LANES : (block + 1) * LANES] = plane.astype(out.dtype)


def edge(acquisitions, valid_dates):
    parts, dates, cols, rows = acquisitions.shape
    blocks = -(-rows // LANES)
    at = (cols - LEFT) // 16
    shape = jax.ShapeDtypeStruct((LEFT, parts, dates, blocks * LANES), acquisitions.dtype)
    return pl.pallas_call(
        functools.partial(edge_kernel, cols - LEFT - at * 16),
        grid=(1,),
        out_shape=shape,
        in_specs=[
            pl.BlockSpec((parts, dates, 16, rows), lambda i: (0, 0, at, 0)),
            pl.BlockSpec((dates, 16, rows), lambda i: (0, at, 0)),
        ],
        out_specs=pl.BlockSpec(shape.shape, lambda i: (0, 0, 0, 0)),
        scratch_shapes=[pltpu.VMEM((parts, blocks, dates * 9, LANES), jnp.float32)],
        compiler_params=pltpu.CompilerParams(vmem_limit_bytes=56 << 20),
        name="edge",
    )(acquisitions, valid_dates)


def pack_kernel(tiles, first_block, blocks, col_groups, segments, axis, *refs):
    acq_refs, refs = refs[:blocks], refs[blocks:]
    valid_refs, refs = refs[:blocks], refs[blocks:]
    halo_ref, refs = refs[0], refs[1:]
    outs, (planes, shifted, halo, sem) = refs[:-4], refs[-4:]
    parts, dates, cols, _ = acq_refs[0].shape
    stride = cols + LEFT
    me = lax.axis_index(axis)
    fetch = pltpu.make_async_copy(halo_ref, halo, sem)
    fetch.start()

    def one_date(date, carry):
        for block in range(blocks):
            keep = valid_refs[block][date].astype(jnp.float32)
            for part in range(parts):
                value = acq_refs[block][part, date].astype(jnp.float32) * keep
                planes[part, block, pl.ds(date * stride, cols)] = value
        return carry

    lax.fori_loop(0, dates, one_date, 0, unroll=4)

    def place(group, block, j, part, plane):
        if j:
            plane = pltpu.roll(plane, TILE_ROWS * j, 1)
        shifted[group, block, j, part] = plane.astype(jnp.bfloat16)

    def one_block(block, carry):
        for group in range(col_groups):
            for j in range(BOX_COLS):
                column = group * STEP_COLS - LEFT + j
                for part in range(parts):
                    if column >= 0:
                        plane = planes[part, block, pl.ds(column, dates, stride=stride), :]
                        place(group, block, j, part, plane)
        return carry

    lax.fori_loop(0, blocks, one_block, 0)
    fetch.wait()
    for block in range(blocks):
        at = (first_block + block) * LANES
        for j in range(LEFT):
            for part in range(parts):
                place(0, block, j, part, halo[j, part, :, at : at + LANES].astype(jnp.float32))
    masks = {}
    for offset, out in enumerate(outs):
        target = me ^ offset
        group = lax.rem(target, col_groups)
        if segments == 1:
            for index, tile in enumerate(tiles):
                total = jnp.zeros((parts * dates // 16, 16, LANES), jnp.bfloat16)
                for j in range(BOX_COLS):
                    row, end = tile * TILE_ROWS, (tile + 1) * TILE_ROWS
                    while row < end:
                        block = row // LANES
                        stop = min(end, (block + 1) * LANES)
                        key = ((row + TILE_ROWS * j) % LANES, stop - row)
                        if key not in masks:
                            masks[key] = lane_mask(*key)
                        piece = shifted[group, block - first_block, j]
                        total = choose(masks[key], piece.reshape(total.shape), total)
                        row = stop
                out[index] = total.reshape(parts, dates, LANES)
        else:
            segment = target // col_groups
            last = segments * len(tiles) - 1

            def one_tile(index, carry):
                tile = segment * len(tiles) + index - 1
                kept = jnp.where((tile >= 0) & (tile <= last), TILE_ROWS, 0)
                row = jnp.clip(tile, 0, last) * TILE_ROWS
                low, high = row // LANES, (row + TILE_ROWS - 1) // LANES
                split = jnp.where(high == low, TILE_ROWS, high * LANES - row)
                total = jnp.zeros((parts * dates // 16, 16, LANES), jnp.bfloat16)
                for j in range(BOX_COLS):
                    start = row + TILE_ROWS * j
                    for block, first, count in (
                        (low, start, jnp.minimum(split, kept)),
                        (high, start + split, jnp.minimum(TILE_ROWS - split, kept)),
                    ):
                        piece = shifted[group, block, j].reshape(total.shape)
                        total = choose(lane_mask(first, count), piece, total)
                out[index] = total.reshape(parts, dates, LANES)
                return carry

            lax.fori_loop(0, len(tiles) + 2, one_tile, 0)


def pack(acquisitions, valid_dates, halo, peers, tiles, col_groups, segments):
    parts, dates, cols, rows = acquisitions.shape
    if segments == 1:
        sent = len(tiles)
        first = tiles[0] * TILE_ROWS // LANES
        blocks = -(-(tiles[-1] + 1) * TILE_ROWS // LANES) - first
    else:
        sent, first, blocks = len(tiles) + 2, 0, -(-rows // LANES)

    def block_specs(shape):
        return [
            pl.BlockSpec(
                shape + (LANES,), functools.partial(lambda b, i: (0,) * len(shape) + (b,), first + k)
            )
            for k in range(blocks)
        ]

    shape = jax.ShapeDtypeStruct((sent, parts, dates, LANES), jnp.bfloat16)
    kernel = functools.partial(pack_kernel, tiles, first, blocks, col_groups, segments, "date")
    return pl.pallas_call(
        kernel,
        grid=(1,),
        out_shape=[shape] * peers,
        in_specs=block_specs((parts, dates, cols))
        + block_specs((dates, cols))
        + [pl.BlockSpec(memory_space=pl.ANY)],
        out_specs=[pl.BlockSpec(shape.shape, lambda i: (0, 0, 0, 0))] * peers,
        scratch_shapes=[
            pltpu.VMEM((parts, blocks, dates * (cols + LEFT), LANES), jnp.float32),
            pltpu.VMEM((col_groups, blocks, BOX_COLS, parts, dates, LANES), jnp.bfloat16),
            pltpu.VMEM(halo.shape, halo.dtype),
            pltpu.SemaphoreType.DMA,
        ],
        compiler_params=pltpu.CompilerParams(vmem_limit_bytes=56 << 20),
        cost_estimate=pl.CostEstimate(
            flops=10**8, bytes_accessed=blocks * 3 * 10**6, transcendentals=0
        ),
        name="pack",
    )(*[acquisitions] * blocks, *[valid_dates] * blocks, halo)


def slot_rows(first):
    lane = lax.broadcasted_iota(jnp.int32, (16, LANES), 1)
    place = (lane - first) & (LANES - 1)
    column = (place * 57) >> 10
    return place - TILE_ROWS * column, column < BOX_COLS


def as_mask(inside):
    return jnp.where(inside, 1.0, 0.0).astype(jnp.bfloat16)[None]


def window_pair(real, imag, k, e, row_now, row_next):
    shape = (-1, 16, LANES)
    begin, spill = STEP_ROWS * e, STEP_ROWS * e + BOX_ROWS - TILE_ROWS
    now, after = row_now >= begin, row_next < spill + STEP_ROWS
    both, a, b = [], real[k].reshape(shape), imag[k].reshape(shape)
    a, b = a * as_mask(now), b * as_mask(now)
    if spill > 0:
        first = as_mask(now | (row_next < spill))
        second = as_mask((row_now >= begin + STEP_ROWS) | after)
        a = a + real[k + 1].reshape(shape) * as_mask(after)
        b = b + imag[k + 1].reshape(shape) * as_mask(after)
    else:
        first = as_mask(now & (row_now < BOX_ROWS))
        second = as_mask(row_now >= STEP_ROWS)
    for window in (first, second):
        parts = [(part * window).reshape(real.shape[1:]) for part in (a, b)]
        both.append(jnp.concatenate(parts, axis=1))
    return a.reshape(real.shape[1:]), b.reshape(real.shape[1:]), both


def coherence_pair(a, b, both, diagonal, held, place):
    count = a.shape[0]
    left = jnp.concatenate(
        [jnp.concatenate([a, b], axis=1), jnp.concatenate([b, -a], axis=1)], axis=0
    )
    sums = lax.dot_general(
        left, jnp.concatenate(both, axis=0), CONTRACT_LAST, preferred_element_type=jnp.float32
    )
    for index in range(2):
        real = sums[:count, index * count : (index + 1) * count]
        imag = sums[count:, index * count : (index + 1) * count]
        energy = jnp.sum(jnp.where(diagonal, real, 0.0), axis=0, keepdims=True) * (1 / NBOX)
        factor = lax.rsqrt(energy + POWER_EPS)
        down = jnp.sum(jnp.where(diagonal, factor, 0.0), axis=1, keepdims=True)
        weights = down * (factor * (1 / NBOX))
        held[place + index, :count] = (real * weights).astype(jnp.bfloat16)
        held[place + index, count:] = (imag * weights).astype(jnp.bfloat16)


def iterate(held, pixels, dates):
    row = lax.broadcasted_iota(jnp.int32, (8, dates), 0)
    odd = (row & 1) == 1
    sign = jnp.where((row & 2) == 2, -1.0, 1.0)
    start = jnp.concatenate([jnp.where(odd, 0.0, sign), jnp.where(odd, -sign, 0.0)], axis=1)
    vectors = [start.astype(jnp.bfloat16)] * pixels
    for sweep in range(ITERS):
        scaled = []
        for place in range(pixels):
            product = jnp.dot(vectors[place], held[place], preferred_element_type=jnp.float32)
            square = product * product
            square = square + pltpu.roll(square, 1, 0)
            total = jnp.sum(square, axis=1, keepdims=True) * (1 / dates) + POWER_EPS
            scaled.append(product * lax.rsqrt(total))
        if sweep + 1 < ITERS:
            vectors = [
                jnp.concatenate([v, pltpu.roll(v, 7, 0)], axis=1).astype(jnp.bfloat16)
                for v in scaled
            ]
    return scaled


def link_kernel(peers, carried, earlier, start, padded, last, *refs):
    sources, refs = refs[:peers], refs[peers:]
    before, refs = refs[: peers * carried], refs[peers * carried :]
    done, refs = refs[:earlier], refs[earlier:]
    outs, (real, imag, held, linked, sems) = refs[:-5], refs[-5:]
    sent, _, dates, _ = sources[0].shape
    all_dates = peers * dates
    base = 0 if padded else 2 if carried else 1
    copies = []

    def fetch(tiles, part, at, peer):
        room = (real, imag)[part].at[pl.ds(at, tiles.shape[0]), pl.ds(peer * dates, dates)]
        copies.append(pltpu.make_async_copy(tiles.at[:, part], room, sems.at[len(copies)]))
        copies[-1].start()

    for peer, source in enumerate(sources):
        for part in range(2):
            fetch(source, part, base, peer)
            if carried:
                tiles = before[peer]
                fetch(tiles.at[pl.ds(tiles.shape[0] - 2, 2)], part, 0, peer)
    zero = jnp.zeros((all_dates, LANES), jnp.bfloat16)
    for tiles in (real, imag):
        if not carried and not padded:
            tiles[0] = zero
        if last and not padded:
            tiles[base + sent] = zero
    for copy in copies:
        copy.wait()
    pixels = linked.shape[0] // 8
    batch = math.gcd(BATCH, pixels)
    diagonal = lax.broadcasted_iota(
        jnp.int32, (all_dates, all_dates), 0
    ) == lax.broadcasted_iota(jnp.int32, (all_dates, all_dates), 1)

    def step(index, carry):
        rows_of = {}

        def rows_at(k):
            if k not in rows_of:
                tile = start // SLOTS - 1 + index * (batch // SLOTS) + k
                if padded:
                    tile = tile + lax.axis_index("date") // padded * (sent - 2)
                row, used = slot_rows(tile * TILE_ROWS)
                rows_of[k] = jnp.where(used, row, -1), jnp.where(used, row, LANES)
            return rows_of[k]

        for place in range(0, batch, 2):
            k, e = divmod(place + SLOTS - LEAD, SLOTS)
            at = index * (batch // SLOTS) + k
            a, b, both = window_pair(real, imag, at, e, rows_at(k)[0], rows_at(k + 1)[1])
            coherence_pair(a, b, both, diagonal, held, place)
        for place, tile in enumerate(iterate(held, batch, all_dates)):
            linked[pl.ds((index * batch + place) * 8, 8)] = tile
        return carry

    lax.fori_loop(0, pixels // batch, step, 0)
    for part in range(2):
        vectors = linked[pl.ds(part, pixels, stride=8), :]
        if not last:
            outs[0][part] = vectors
            continue
        vectors = jnp.concatenate([ref[part] for ref in done] + [vectors], axis=0)
        flat = jnp.transpose(vectors)
        for peer, out in enumerate(outs):
            out[part] = flat[peer * dates : (peer + 1) * dates]


def link(sources, before, done, start, pixels, padded, last):
    peers = len(sources)
    sent, parts, dates, _ = sources[0].shape
    all_dates = peers * dates
    whole = pl.BlockSpec(memory_space=pltpu.VMEM)
    operands = list(sources) + list(before)
    specs = [pl.BlockSpec(memory_space=pl.ANY)] * len(operands)
    operands += done
    specs += [whole] * len(done)
    if last:
        rows = start + pixels
        outs = [jax.ShapeDtypeStruct((parts, dates, rows), jnp.float32)] * peers
    else:
        outs = [jax.ShapeDtypeStruct((parts, pixels, all_dates), jnp.float32)]
    kept = sent + 3
    kernel = functools.partial(
        link_kernel, peers, len(before) > 0, len(done), start, padded, last
    )
    return pl.pallas_call(
        kernel,
        grid=(1,),
        out_shape=outs,
        in_specs=specs,
        out_specs=[whole] * len(outs),
        scratch_shapes=[
            pltpu.VMEM((kept, all_dates, LANES), jnp.bfloat16),
            pltpu.VMEM((kept, all_dates, LANES), jnp.bfloat16),
            pltpu.VMEM((math.gcd(BATCH, pixels), 2 * all_dates, all_dates), jnp.bfloat16),
            pltpu.VMEM((pixels * 8, all_dates), jnp.float32),
            pltpu.SemaphoreType.DMA((4 * peers,)),
        ],
        compiler_params=pltpu.CompilerParams(vmem_limit_bytes=56 << 20),
        cost_estimate=pl.CostEstimate(
            flops=pixels * 30 * 10**6, bytes_accessed=10**6, transcendentals=0
        ),
        name="link",
    )(*operands)


def swap(blocks, axis):
    count = len(blocks)
    return [blocks[0]] + [
        lax.ppermute(blocks[m], axis, [(i, i ^ m) for i in range(count)]) for m in range(1, count)
    ]


def place_kernel(peers, out_cols, *refs):
    blocks, out = refs[:peers], refs[peers]
    rows = blocks[0].shape[2]
    me = lax.axis_index("date")
    for target in range(peers):
        value = blocks[target][...]
        for other in range(1, peers):
            value = jnp.where(me == other, blocks[target ^ other][...], value)
        segment = target // out_cols * rows
        out[:, :, target % out_cols, segment : segment + rows] = value


def place_blocks(blocks, out_cols, segments):
    parts, dates, rows = blocks[0].shape
    whole = pl.BlockSpec(memory_space=pltpu.VMEM)
    return pl.pallas_call(
        functools.partial(place_kernel, len(blocks), out_cols),
        out_shape=jax.ShapeDtypeStruct((parts, dates, out_cols, rows * segments), jnp.float32),
        in_specs=[whole] * len(blocks),
        out_specs=whole,
        compiler_params=pltpu.CompilerParams(vmem_limit_bytes=56 << 20),
        name="place",
    )(*blocks)


def chunk_ends(tiles, segments):
    step = BATCH // SLOTS
    if segments > 1 or tiles % step:
        return [tiles]
    count = tiles // step
    return [step * (count * share // 8) + 1 for share in CHUNKS] + [tiles]


def on_device(acquisitions, valid_dates):
    peers = lax.axis_size("date")
    strips = lax.axis_size("space")
    parts, dates, cols, rows = acquisitions.shape
    out_cols = cols // STEP_COLS
    segments = peers // out_cols
    tiles = rows // TILE_ROWS // segments
    pixels = rows // STEP_ROWS // segments
    halo = lax.ppermute(
        edge(acquisitions, valid_dates), "space", [(i, i + 1) for i in range(strips - 1)]
    )
    ends = chunk_ends(tiles, segments)
    outgoing = [
        pack(acquisitions, valid_dates, halo, peers, range(low, high), out_cols, segments)
        for low, high in zip([0] + ends[:-1], ends)
    ]
    incoming = [swap(blocks, "date") for blocks in outgoing]
    done, start = [], 0
    for index, blocks in enumerate(incoming):
        last = index == len(ends) - 1
        stop = pixels if last else (ends[index] - 1) * SLOTS
        before = incoming[index - 1] if index else []
        result = link(
            blocks, before, done if last else [], start, stop - start,
            0 if segments == 1 else out_cols, last,
        )
        done, start = done + list(result), stop
    incoming = swap(result, "date")
    return place_blocks(incoming, out_cols, segments)


def solution(mesh):
    in_specs = (P(None, "date", "space", None), P("date", "space", None))
    out_specs = P(None, "date", "space", None)
    return jax.shard_map(
        on_device, mesh=mesh, in_specs=in_specs, out_specs=out_specs, check_vma=False
    )
```

```python
import functools
import math

import jax
import jax.numpy as jnp
from jax import lax
from jax.experimental import pallas as pl
from jax.experimental.pallas import tpu as pltpu
from jax.sharding import PartitionSpec as P

BOX_ROWS = 15
BOX_COLS = 7
STEP_ROWS = 3
STEP_COLS = 6
ITERS = 4
MARGIN = 6
NBOX = 105
POWER_EPS = 1e-05

LANES = 128
TILE_ROWS = 18
SLOTS = TILE_ROWS // STEP_ROWS
LEAD = MARGIN // STEP_ROWS
LEFT = STEP_COLS // 2
BATCH = 48
CHUNKS = (4,)
CONTRACT_LAST = (((1,), (1,)), ((), ()))


def lane_mask(first, count):
    lane = lax.broadcasted_iota(jnp.int32, (16, LANES), 1)
    inside = ((lane - first) & (LANES - 1)) < count
    return (jnp.where(inside, 1.0, 0.0).astype(jnp.bfloat16) > 0)[None]


def choose(mask, yes, no):
    return jnp.where(jnp.broadcast_to(mask, yes.shape), yes, no)


def edge_kernel(first, *refs):
    acq_ref, valid_ref, out, planes = refs
    parts, dates, _, rows = acq_ref.shape
    stride = planes.shape[2] // dates
    span = slice(first // 8 * 8, first // 8 * 8 + 8)
    offset = first % 8

    def one_date(date, carry):
        keep = valid_ref[date, span].astype(jnp.float32)
        for part in range(parts):
            value = acq_ref[part, date, span].astype(jnp.float32) * keep
            for block in range(planes.shape[1]):
                width = min(LANES, rows - block * LANES)
                planes[part, block, pl.ds(date * stride, 8), :width] = value[
                    :, block * LANES : block * LANES + width
                ]
        return carry

    for part in range(parts):
        planes[part, planes.shape[1] - 1] = jnp.zeros(planes.shape[2:], jnp.float32)
    lax.fori_loop(0, dates, one_date, 0, unroll=4)
    for j in range(LEFT):
        for part in range(parts):
            for block in range(planes.shape[1]):
                plane = planes[part, block, pl.ds(offset + j, dates, stride=stride), :]
                out[j, part, :, block * LANES : (block + 1) * LANES] = plane.astype(out.dtype)


def edge(acquisitions, valid_dates):
    parts, dates, cols, rows = acquisitions.shape
    blocks = -(-rows // LANES)
    at = (cols - LEFT) // 16
    shape = jax.ShapeDtypeStruct((LEFT, parts, dates, blocks * LANES), acquisitions.dtype)
    return pl.pallas_call(
        functools.partial(edge_kernel, cols - LEFT - at * 16),
        grid=(1,),
        out_shape=shape,
        in_specs=[
            pl.BlockSpec((parts, dates, 16, rows), lambda i: (0, 0, at, 0)),
            pl.BlockSpec((dates, 16, rows), lambda i: (0, at, 0)),
        ],
        out_specs=pl.BlockSpec(shape.shape, lambda i: (0, 0, 0, 0)),
        scratch_shapes=[pltpu.VMEM((parts, blocks, dates * 9, LANES), jnp.float32)],
        compiler_params=pltpu.CompilerParams(vmem_limit_bytes=16 << 20),
        name="edge",
    )(acquisitions, valid_dates)


def turn(plane, j):
    return pltpu.roll(plane, TILE_ROWS * j, 1) if j else plane


def edge_planes(halo, first_block, blocks, keep):
    for block in range(blocks):
        at = (first_block + block) * LANES
        for j in range(LEFT):
            for part in range(halo.shape[1]):
                plane = halo[j, part, :, at : at + LANES].astype(jnp.float32)
                keep(block, j, part, turn(plane, j).astype(jnp.bfloat16))


def compose(total, tile, columns, piece, masks):
    for j in columns:
        row, end = tile * TILE_ROWS, (tile + 1) * TILE_ROWS
        while row < end:
            block = row // LANES
            stop = min(end, (block + 1) * LANES)
            key = ((row + TILE_ROWS * j) % LANES, stop - row)
            if key not in masks:
                masks[key] = lane_mask(*key)
            total = choose(masks[key], piece(block, j).reshape(total.shape), total)
            row = stop
    return total


def compose_at(total, tile, last, columns, piece):
    kept = jnp.where((tile >= 0) & (tile <= last), TILE_ROWS, 0)
    row = jnp.clip(tile, 0, last) * TILE_ROWS
    low, high = row // LANES, (row + TILE_ROWS - 1) // LANES
    split = jnp.where(high == low, TILE_ROWS, high * LANES - row)
    for j in columns:
        start = row + TILE_ROWS * j
        for block, first, count in (
            (low, start, jnp.minimum(split, kept)),
            (high, start + split, jnp.minimum(TILE_ROWS - split, kept)),
        ):
            total = choose(lane_mask(first, count), piece(block, j).reshape(total.shape), total)
    return total


def pack_kernel(ends, first_block, blocks, col_groups, segments, with_halo, *refs):
    acq_refs, refs = refs[:blocks], refs[blocks:]
    valid_refs, refs = refs[:blocks], refs[blocks:]
    if with_halo:
        halo_ref, refs = refs[0], refs[1:]
        refs, (halo, sem) = refs[:-2], refs[-2:]
        fetch = pltpu.make_async_copy(halo_ref, halo, sem)
        fetch.start()
    outs, (planes, shifted) = refs[:-2], refs[-2:]
    parts, dates, cols, _ = acq_refs[0].shape
    stride = planes.shape[2] // dates
    me = lax.axis_index("date")

    def one_date(date, carry):
        for block in range(blocks):
            keep = valid_refs[block][date].astype(jnp.float32)
            for part in range(parts):
                value = acq_refs[block][part, date].astype(jnp.float32) * keep
                planes[part, block, pl.ds(date * stride, cols)] = value
        return carry

    lax.fori_loop(0, dates, one_date, 0, unroll=4)

    def one_block(block, carry):
        for group in range(col_groups):
            for j in range(BOX_COLS):
                column = group * STEP_COLS - LEFT + j
                for part in range(parts):
                    if column >= 0:
                        plane = planes[part, block, pl.ds(column, dates, stride=stride), :]
                        shifted[group, block, j, part] = turn(plane, j).astype(jnp.bfloat16)
        return carry

    lax.fori_loop(0, blocks, one_block, 0)

    def keep_edge(block, j, part, plane):
        shifted[0, block, j, part] = plane

    if with_halo:
        fetch.wait()
        edge_planes(halo, first_block, blocks, keep_edge)
    else:
        zero = jnp.zeros((dates, LANES), jnp.bfloat16)
        for block in range(blocks):
            for j in range(LEFT):
                for part in range(parts):
                    keep_edge(block, j, part, zero)
    masks = {}
    chunks = len(ends) - 1
    empty = jnp.zeros((parts * dates // 16, 16, LANES), jnp.bfloat16)
    for offset in range(len(outs) // chunks):
        mine = outs[offset * chunks : (offset + 1) * chunks]
        target = me ^ offset
        group = lax.rem(target, col_groups)

        def piece(block, j):
            return shifted[group, block - first_block, j]

        if segments == 1:
            for tile in range(ends[0], ends[-1]):
                chunk = sum(tile >= end for end in ends[1:])
                total = compose(empty, tile, range(BOX_COLS), piece, masks)
                mine[chunk][tile - ends[chunk]] = total.reshape(parts, dates, LANES)
        else:
            tiles, segment = ends[-1], target // col_groups

            def one_tile(index, carry):
                tile, last = segment * tiles + index - 1, segments * tiles - 1
                total = compose_at(empty, tile, last, range(BOX_COLS), piece)
                mine[0][index] = total.reshape(parts, dates, LANES)
                return carry

            lax.fori_loop(0, tiles + 2, one_tile, 0)


def pack(acquisitions, valid_dates, halo, peers, ends, col_groups, segments):
    parts, dates, cols, rows = acquisitions.shape
    if segments == 1:
        sent = [high - low for low, high in zip(ends, ends[1:])]
        first = ends[0] * TILE_ROWS // LANES
        blocks = -(-ends[-1] * TILE_ROWS // LANES) - first
    else:
        sent, first, blocks = [ends[-1] + 2], 0, -(-rows // LANES)

    def block_specs(shape):
        return [
            pl.BlockSpec(
                shape + (LANES,), functools.partial(lambda b, i: (0,) * len(shape) + (b,), first + k)
            )
            for k in range(blocks)
        ]

    chunks = len(sent)
    shapes = [jax.ShapeDtypeStruct((n, parts, dates, LANES), jnp.bfloat16) for n in sent]
    operands = [acquisitions] * blocks + [valid_dates] * blocks
    specs = block_specs((parts, dates, cols)) + block_specs((dates, cols))
    scratch = [
        pltpu.VMEM((parts, blocks, dates * (cols + 1), LANES), jnp.float32),
        pltpu.VMEM((col_groups, blocks, BOX_COLS, parts, dates, LANES), jnp.bfloat16),
    ]
    if halo is not None:
        operands.append(halo)
        specs.append(pl.BlockSpec(memory_space=pl.ANY))
        scratch += [pltpu.VMEM(halo.shape, halo.dtype), pltpu.SemaphoreType.DMA]
    outs = pl.pallas_call(
        functools.partial(
            pack_kernel, ends, first, blocks, col_groups, segments, halo is not None
        ),
        grid=(1,),
        out_shape=shapes * peers,
        in_specs=specs,
        out_specs=[pl.BlockSpec(memory_space=pltpu.VMEM)] * (peers * chunks),
        scratch_shapes=scratch,
        compiler_params=pltpu.CompilerParams(vmem_limit_bytes=36 << 20),
        cost_estimate=pl.CostEstimate(
            flops=10**8, bytes_accessed=blocks * 3 * 10**6, transcendentals=0
        ),
        name="pack",
    )(*operands)
    return [list(outs[chunk::chunks]) for chunk in range(chunks)]


def patch_kernel(tiles, col_groups, segments, *refs):
    halo_ref, refs = refs[0], refs[1:]
    peers = (len(refs) - 4) // 2
    outs, (halo, planes, held, sems) = refs[peers:-4], refs[-4:]
    sent, parts, dates, _ = held.shape
    blocks = planes.shape[0]
    me = lax.axis_index("date")
    fetch = pltpu.make_async_copy(halo_ref, halo, sems.at[0])
    fetch.start()
    shape = (parts * dates // 16, 16, LANES)

    def keep_edge(block, j, part, plane):
        planes[block, j, part] = plane

    def piece(block, j):
        return planes[block, j]

    for offset, out in enumerate(outs):
        target = me ^ offset

        @pl.when(lax.rem(target, col_groups) == 0)
        def _(out=out, target=target):
            read = pltpu.make_async_copy(out, held, sems.at[1])
            read.start()
            if offset < col_groups:
                fetch.wait()
                edge_planes(halo, 0, blocks, keep_edge)
            read.wait()
            masks = {}
            if segments == 1:
                for tile in range(tiles):
                    total = held[tile].reshape(shape)
                    total = compose(total, tile, range(LEFT), piece, masks)
                    held[tile] = total.reshape(held.shape[1:])
            else:
                segment = target // col_groups

                def one_tile(index, carry):
                    tile, last = segment * tiles + index - 1, segments * tiles - 1
                    total = held[index].reshape(shape)
                    total = compose_at(total, tile, last, range(LEFT), piece)
                    held[index] = total.reshape(held.shape[1:])
                    return carry

                lax.fori_loop(0, sent, one_tile, 0)
            write = pltpu.make_async_copy(held, out, sems.at[2])
            write.start()
            write.wait()


def patch(blocks, halo, tiles, col_groups, segments):
    peers = len(blocks)
    _, parts, dates, _ = blocks[0].shape
    if segments == 1:
        lanes = -(-tiles * TILE_ROWS // LANES)
    else:
        lanes = halo.shape[3] // LANES
    anywhere = pl.BlockSpec(memory_space=pl.ANY)
    return pl.pallas_call(
        functools.partial(patch_kernel, tiles, col_groups, segments),
        out_shape=[jax.ShapeDtypeStruct(block.shape, block.dtype) for block in blocks],
        in_specs=[anywhere] * (1 + peers),
        out_specs=[anywhere] * peers,
        scratch_shapes=[
            pltpu.VMEM(halo.shape, halo.dtype),
            pltpu.VMEM((lanes, LEFT, parts, dates, LANES), jnp.bfloat16),
            pltpu.VMEM(blocks[0].shape, jnp.bfloat16),
            pltpu.SemaphoreType.DMA((3,)),
        ],
        input_output_aliases={1 + m: m for m in range(peers)},
        compiler_params=pltpu.CompilerParams(vmem_limit_bytes=16 << 20),
        name="patch",
    )(halo, *blocks)


def slot_rows(first):
    lane = lax.broadcasted_iota(jnp.int32, (16, LANES), 1)
    place = (lane - first) & (LANES - 1)
    column = (place * 57) >> 10
    return place - TILE_ROWS * column, column < BOX_COLS


def as_mask(inside):
    return jnp.where(inside, 1.0, 0.0).astype(jnp.bfloat16)[None]


def window_pair(real, imag, k, e, row_now, row_next):
    shape = (-1, 16, LANES)
    begin, spill = STEP_ROWS * e, STEP_ROWS * e + BOX_ROWS - TILE_ROWS
    now, after = row_now >= begin, row_next < spill + STEP_ROWS
    both, a, b = [], real[k].reshape(shape), imag[k].reshape(shape)
    a, b = a * as_mask(now), b * as_mask(now)
    if spill > 0:
        first = as_mask(now | (row_next < spill))
        second = as_mask((row_now >= begin + STEP_ROWS) | after)
        a = a + real[k + 1].reshape(shape) * as_mask(after)
        b = b + imag[k + 1].reshape(shape) * as_mask(after)
    else:
        first = as_mask(now & (row_now < BOX_ROWS))
        second = as_mask(row_now >= STEP_ROWS)
    for window in (first, second):
        parts = [(part * window).reshape(real.shape[1:]) for part in (a, b)]
        both.append(jnp.concatenate(parts, axis=1))
    return a.reshape(real.shape[1:]), b.reshape(real.shape[1:]), both


def coherence_pair(a, b, both, diagonal, held, place):
    count = a.shape[0]
    left = jnp.concatenate(
        [jnp.concatenate([a, b], axis=1), jnp.concatenate([b, -a], axis=1)], axis=0
    )
    sums = lax.dot_general(
        left, jnp.concatenate(both, axis=0), CONTRACT_LAST, preferred_element_type=jnp.float32
    )
    for index in range(2):
        real = sums[:count, index * count : (index + 1) * count]
        imag = sums[count:, index * count : (index + 1) * count]
        energy = jnp.sum(jnp.where(diagonal, real, 0.0), axis=0, keepdims=True) * (1 / NBOX)
        factor = lax.rsqrt(energy + POWER_EPS)
        down = jnp.sum(jnp.where(diagonal, factor, 0.0), axis=1, keepdims=True)
        weights = down * (factor * (1 / NBOX))
        held[place + index, :count] = (real * weights).astype(jnp.bfloat16)
        held[place + index, count:] = (imag * weights).astype(jnp.bfloat16)


def iterate(held, pixels, dates):
    row = lax.broadcasted_iota(jnp.int32, (8, dates), 0)
    odd = (row & 1) == 1
    sign = jnp.where((row & 2) == 2, -1.0, 1.0)
    start = jnp.concatenate([jnp.where(odd, 0.0, sign), jnp.where(odd, -sign, 0.0)], axis=1)
    vectors = [start.astype(jnp.bfloat16)] * pixels
    for sweep in range(ITERS):
        scaled = []
        for place in range(pixels):
            product = jnp.dot(vectors[place], held[place], preferred_element_type=jnp.float32)
            square = product * product
            square = square + pltpu.roll(square, 1, 0)
            total = jnp.sum(square, axis=1, keepdims=True) * (1 / dates) + POWER_EPS
            scaled.append(product * lax.rsqrt(total))
        if sweep + 1 < ITERS:
            vectors = [
                jnp.concatenate([v, pltpu.roll(v, 7, 0)], axis=1).astype(jnp.bfloat16)
                for v in scaled
            ]
    return scaled


def link_kernel(peers, carried, earlier, start, padded, last, *refs):
    sources, refs = refs[:peers], refs[peers:]
    before, refs = refs[: peers * carried], refs[peers * carried :]
    done, refs = refs[:earlier], refs[earlier:]
    outs, (real, imag, held, linked, sems) = refs[:-5], refs[-5:]
    sent, _, dates, _ = sources[0].shape
    all_dates = peers * dates
    base = 0 if padded else 2 if carried else 1
    copies = []

    def fetch(tiles, part, at, peer):
        room = (real, imag)[part].at[pl.ds(at, tiles.shape[0]), pl.ds(peer * dates, dates)]
        copies.append(pltpu.make_async_copy(tiles.at[:, part], room, sems.at[len(copies)]))
        copies[-1].start()

    for peer, source in enumerate(sources):
        for part in range(2):
            fetch(source, part, base, peer)
            if carried:
                tiles = before[peer]
                fetch(tiles.at[pl.ds(tiles.shape[0] - 2, 2)], part, 0, peer)
    zero = jnp.zeros((all_dates, LANES), jnp.bfloat16)
    for tiles in (real, imag):
        if not carried and not padded:
            tiles[0] = zero
        if last and not padded:
            tiles[base + sent] = zero
    for copy in copies:
        copy.wait()
    pixels = linked.shape[1]
    batch = math.gcd(BATCH, pixels)
    diagonal = lax.broadcasted_iota(
        jnp.int32, (all_dates, all_dates), 0
    ) == lax.broadcasted_iota(jnp.int32, (all_dates, all_dates), 1)

    def step(index, carry):
        rows_of = {}

        def rows_at(k):
            if k not in rows_of:
                tile = start // SLOTS - 1 + index * (batch // SLOTS) + k
                if padded:
                    tile = tile + lax.axis_index("date") // padded * (sent - 2)
                row, used = slot_rows(tile * TILE_ROWS)
                rows_of[k] = jnp.where(used, row, -1), jnp.where(used, row, LANES)
            return rows_of[k]

        for place in range(0, batch, 2):
            k, e = divmod(place + SLOTS - LEAD, SLOTS)
            at = index * (batch // SLOTS) + k
            a, b, both = window_pair(real, imag, at, e, rows_at(k)[0], rows_at(k + 1)[1])
            coherence_pair(a, b, both, diagonal, held, place)
        for place, tile in enumerate(iterate(held, batch, all_dates)):
            for part in range(2):
                linked[part, pl.ds(index * batch + place, 1)] = tile[part : part + 1]
        return carry

    lax.fori_loop(0, pixels // batch, step, 0)
    for part in range(2):
        vectors = linked[part]
        if not last:
            outs[0][part] = vectors
            continue
        vectors = jnp.concatenate([ref[part] for ref in done] + [vectors], axis=0)
        flat = jnp.transpose(vectors)
        for peer, out in enumerate(outs):
            out[part] = flat[peer * dates : (peer + 1) * dates]


def link(sources, before, done, start, pixels, padded, last):
    peers = len(sources)
    sent, parts, dates, _ = sources[0].shape
    all_dates = peers * dates
    whole = pl.BlockSpec(memory_space=pltpu.VMEM)
    operands = list(sources) + list(before)
    specs = [pl.BlockSpec(memory_space=pl.ANY)] * len(operands)
    operands += done
    specs += [whole] * len(done)
    if last:
        rows = start + pixels
        outs = [jax.ShapeDtypeStruct((parts, dates, rows), jnp.float32)] * peers
    else:
        outs = [jax.ShapeDtypeStruct((parts, pixels, all_dates), jnp.float32)]
    kept = sent + 3
    kernel = functools.partial(
        link_kernel, peers, len(before) > 0, len(done), start, padded, last
    )
    return pl.pallas_call(
        kernel,
        grid=(1,),
        out_shape=outs,
        in_specs=specs,
        out_specs=[whole] * len(outs),
        scratch_shapes=[
            pltpu.VMEM((kept, all_dates, LANES), jnp.bfloat16),
            pltpu.VMEM((kept, all_dates, LANES), jnp.bfloat16),
            pltpu.VMEM((math.gcd(BATCH, pixels), 2 * all_dates, all_dates), jnp.bfloat16),
            pltpu.VMEM((2, pixels, all_dates), jnp.float32),
            pltpu.SemaphoreType.DMA((4 * peers,)),
        ],
        compiler_params=pltpu.CompilerParams(vmem_limit_bytes=20 << 20),
        cost_estimate=pl.CostEstimate(
            flops=pixels * 30 * 10**6, bytes_accessed=10**6, transcendentals=0
        ),
        name="link",
    )(*operands)


def swap(blocks, axis):
    count = len(blocks)
    return [blocks[0]] + [
        lax.ppermute(blocks[m], axis, [(i, i ^ m) for i in range(count)]) for m in range(1, count)
    ]


def place_kernel(peers, out_cols, *refs):
    blocks, out = refs[:peers], refs[peers]
    rows = blocks[0].shape[2]
    me = lax.axis_index("date")
    for target in range(peers):
        value = blocks[target][...]
        for other in range(1, peers):
            value = jnp.where(me == other, blocks[target ^ other][...], value)
        segment = target // out_cols * rows
        out[:, :, target % out_cols, segment : segment + rows] = value


def place_blocks(blocks, out_cols, segments):
    parts, dates, rows = blocks[0].shape
    whole = pl.BlockSpec(memory_space=pltpu.VMEM)
    return pl.pallas_call(
        functools.partial(place_kernel, len(blocks), out_cols),
        out_shape=jax.ShapeDtypeStruct((parts, dates, out_cols, rows * segments), jnp.float32),
        in_specs=[whole] * len(blocks),
        out_specs=whole,
        compiler_params=pltpu.CompilerParams(vmem_limit_bytes=8 << 20),
        name="place",
    )(*blocks)


def chunk_ends(tiles, segments):
    step = BATCH // SLOTS
    if segments > 1 or tiles % step:
        return [tiles]
    count = tiles // step
    return [step * (count * share // 8) + 1 for share in CHUNKS] + [tiles]


def on_device(acquisitions, valid_dates):
    peers = lax.axis_size("date")
    strips = lax.axis_size("space")
    parts, dates, cols, rows = acquisitions.shape
    out_cols = cols // STEP_COLS
    segments = peers // out_cols
    tiles = rows // TILE_ROWS // segments
    pixels = rows // STEP_ROWS // segments
    halo = lax.ppermute(
        edge(acquisitions, valid_dates), "space", [(i, i + 1) for i in range(strips - 1)]
    )
    ends = chunk_ends(tiles, segments)
    first, *rest = ends
    (blocks,) = pack(acquisitions, valid_dates, None, peers, [0, first], out_cols, segments)
    outgoing = [patch(blocks, halo, first, out_cols, segments)]
    if rest:
        outgoing += pack(acquisitions, valid_dates, halo, peers, ends, out_cols, segments)
    incoming = [swap(blocks, "date") for blocks in outgoing]
    done, start = [], 0
    for index, blocks in enumerate(incoming):
        last = index == len(ends) - 1
        stop = pixels if last else (ends[index] - 1) * SLOTS
        before = incoming[index - 1] if index else []
        result = link(
            blocks, before, done if last else [], start, stop - start,
            0 if segments == 1 else out_cols, last,
        )
        done, start = done + list(result), stop
    incoming = swap(result, "date")
    return place_blocks(incoming, out_cols, segments)


def solution(mesh):
    in_specs = (P(None, "date", "space", None), P("date", "space", None))
    out_specs = P(None, "date", "space", None)
    return jax.shard_map(
        on_device, mesh=mesh, in_specs=in_specs, out_specs=out_specs, check_vma=False
    )
```

```python
import functools

import jax
import jax.numpy as jnp
from jax import lax
from jax.experimental import pallas as pl
from jax.experimental.pallas import tpu as pltpu
from jax.sharding import PartitionSpec as P

BOX_ROWS = 15
BOX_COLS = 7
STEP_ROWS = 3
STEP_COLS = 6
ITERS = 4
MARGIN = 6
NBOX = 105
POWER_EPS = 1e-05

LANES = 128
TILE_ROWS = 18
SLOTS = TILE_ROWS // STEP_ROWS
LEAD = MARGIN // STEP_ROWS
LEFT = STEP_COLS // 2
BATCH = 60
FIRST = 19
CONTRACT_LAST = (((1,), (1,)), ((), ()))


def lane_mask(first, count):
    lane = lax.broadcasted_iota(jnp.int32, (16, LANES), 1)
    inside = ((lane - first) & (LANES - 1)) < count
    return (jnp.where(inside, 1.0, 0.0).astype(jnp.bfloat16) > 0)[None]


def choose(mask, yes, no):
    return jnp.where(jnp.broadcast_to(mask, yes.shape), yes, no)


def edge_kernel(first, ranges, *refs):
    acq_ref, valid_ref, *outs, planes = refs
    parts, dates, _, rows = acq_ref.shape
    stride = planes.shape[2] // dates
    span = slice(first // 8 * 8, first // 8 * 8 + 8)
    offset = first % 8

    def one_date(date, carry):
        keep = valid_ref[date, span].astype(jnp.float32)
        for part in range(parts):
            value = acq_ref[part, date, span].astype(jnp.float32) * keep
            for block in range(planes.shape[1]):
                width = min(LANES, rows - block * LANES)
                planes[part, block, pl.ds(date * stride, 8), :width] = value[
                    :, block * LANES : block * LANES + width
                ]
        return carry

    for part in range(parts):
        planes[part, planes.shape[1] - 1] = jnp.zeros(planes.shape[2:], jnp.float32)
    lax.fori_loop(0, dates, one_date, 0, unroll=4)
    for j in range(LEFT):
        for part in range(parts):
            for out, span in zip(outs, ranges):
                for index, block in enumerate(span):
                    plane = planes[part, block, pl.ds(offset + j, dates, stride=stride), :]
                    lanes = slice(index * LANES, (index + 1) * LANES)
                    out[j, part, :, lanes] = plane.astype(out.dtype)


def edge(acquisitions, valid_dates, ranges):
    parts, dates, cols, rows = acquisitions.shape
    blocks = -(-rows // LANES)
    at = (cols - LEFT) // 16
    shapes = [
        jax.ShapeDtypeStruct((LEFT, parts, dates, len(span) * LANES), acquisitions.dtype)
        for span in ranges
    ]
    return pl.pallas_call(
        functools.partial(edge_kernel, cols - LEFT - at * 16, ranges),
        grid=(1,),
        out_shape=shapes,
        in_specs=[
            pl.BlockSpec((parts, dates, 16, rows), lambda i: (0, 0, at, 0)),
            pl.BlockSpec((dates, 16, rows), lambda i: (0, at, 0)),
        ],
        out_specs=[pl.BlockSpec(shape.shape, lambda i: (0, 0, 0, 0)) for shape in shapes],
        scratch_shapes=[pltpu.VMEM((parts, blocks, dates * 9, LANES), jnp.float32)],
        compiler_params=pltpu.CompilerParams(vmem_limit_bytes=60 << 20),
        name="edge",
    )(acquisitions, valid_dates)


def turn(plane, j):
    return pltpu.roll(plane, TILE_ROWS * j, 1) if j else plane


def edge_planes(halo, keep):
    for block in range(halo.shape[3] // LANES):
        at = block * LANES
        for j in range(LEFT):
            for part in range(halo.shape[1]):
                plane = halo[j, part, :, at : at + LANES].astype(jnp.float32)
                keep(block, j, part, turn(plane, j).astype(jnp.bfloat16))


def compose(total, tile, columns, piece, masks):
    for j in columns:
        row, end = tile * TILE_ROWS, (tile + 1) * TILE_ROWS
        while row < end:
            block = row // LANES
            stop = min(end, (block + 1) * LANES)
            key = ((row + TILE_ROWS * j) % LANES, stop - row)
            if key not in masks:
                masks[key] = lane_mask(*key)
            total = choose(masks[key], piece(block, j).reshape(total.shape), total)
            row = stop
    return total


def compose_at(total, tile, last, columns, piece):
    kept = jnp.where((tile >= 0) & (tile <= last), TILE_ROWS, 0)
    row = jnp.clip(tile, 0, last) * TILE_ROWS
    low, high = row // LANES, (row + TILE_ROWS - 1) // LANES
    split = jnp.where(high == low, TILE_ROWS, high * LANES - row)
    for j in columns:
        start = row + TILE_ROWS * j
        for block, first, count in (
            (low, start, jnp.minimum(split, kept)),
            (high, start + split, jnp.minimum(TILE_ROWS - split, kept)),
        ):
            total = choose(lane_mask(first, count), piece(block, j).reshape(total.shape), total)
    return total


def pack_kernel(ends, first_block, blocks, col_groups, segments, with_halo, *refs):
    acq_refs, refs = refs[:blocks], refs[blocks:]
    valid_refs, refs = refs[:blocks], refs[blocks:]
    if with_halo:
        halo_ref, refs = refs[0], refs[1:]
        refs, (halo, sem) = refs[:-2], refs[-2:]
        fetch = pltpu.make_async_copy(halo_ref, halo, sem)
        fetch.start()
    outs, (planes, shifted) = refs[:-2], refs[-2:]
    parts, dates, cols, _ = acq_refs[0].shape
    stride = planes.shape[2] // dates
    me = lax.axis_index("date")

    def one_date(date, carry):
        for block in range(blocks):
            keep = valid_refs[block][date].astype(jnp.float32)
            for part in range(parts):
                value = acq_refs[block][part, date].astype(jnp.float32) * keep
                planes[part, block, pl.ds(date * stride, cols)] = value
        return carry

    lax.fori_loop(0, dates, one_date, 0, unroll=4)

    def one_block(block, carry):
        for group in range(col_groups):
            for j in range(BOX_COLS):
                column = group * STEP_COLS - LEFT + j
                for part in range(parts):
                    if column >= 0:
                        plane = planes[part, block, pl.ds(column, dates, stride=stride), :]
                        shifted[group, block, j, part] = turn(plane, j).astype(jnp.bfloat16)
        return carry

    lax.fori_loop(0, blocks, one_block, 0)

    def keep_edge(block, j, part, plane):
        shifted[0, block, j, part] = plane

    if with_halo:
        fetch.wait()
        edge_planes(halo, keep_edge)
    else:
        zero = jnp.zeros((dates, LANES), jnp.bfloat16)
        for block in range(blocks):
            for j in range(LEFT):
                for part in range(parts):
                    keep_edge(block, j, part, zero)
    masks = {}
    chunks = len(ends) - 1
    empty = jnp.zeros((parts * dates // 16, 16, LANES), jnp.bfloat16)
    for offset in range(len(outs) // chunks):
        mine = outs[offset * chunks : (offset + 1) * chunks]
        target = me ^ offset
        group = lax.rem(target, col_groups)

        def piece(block, j):
            return shifted[group, block - first_block, j]

        if segments == 1:
            for tile in range(ends[0], ends[-1]):
                chunk = sum(tile >= end for end in ends[1:])
                total = compose(empty, tile, range(BOX_COLS), piece, masks)
                mine[chunk][tile - ends[chunk]] = total.reshape(parts, dates, LANES)
        else:
            tiles, segment = ends[-1], target // col_groups

            def one_tile(index, carry):
                tile, last = segment * tiles + index - 1, segments * tiles - 1
                total = compose_at(empty, tile, last, range(BOX_COLS), piece)
                mine[0][index] = total.reshape(parts, dates, LANES)
                return carry

            lax.fori_loop(0, tiles + 2, one_tile, 0)


def blocks_of(low, high, rows, segments):
    if segments > 1:
        return range(-(-rows // LANES))
    return range(low * TILE_ROWS // LANES, -(-high * TILE_ROWS // LANES))


def pack(acquisitions, valid_dates, halo, peers, ends, col_groups, segments):
    parts, dates, cols, rows = acquisitions.shape
    span = blocks_of(ends[0], ends[-1], rows, segments)
    first, blocks = span[0], len(span)
    sent = [high - low + (2 if segments > 1 else 0) for low, high in zip(ends, ends[1:])]

    def block_specs(shape):
        return [
            pl.BlockSpec(
                shape + (LANES,), functools.partial(lambda b, i: (0,) * len(shape) + (b,), first + k)
            )
            for k in range(blocks)
        ]

    chunks = len(sent)
    shapes = [jax.ShapeDtypeStruct((n, parts, dates, LANES), jnp.bfloat16) for n in sent]
    operands = [acquisitions] * blocks + [valid_dates] * blocks
    specs = block_specs((parts, dates, cols)) + block_specs((dates, cols))
    scratch = [
        pltpu.VMEM((parts, blocks, dates * (cols + 1), LANES), jnp.float32),
        pltpu.VMEM((col_groups, blocks, BOX_COLS, parts, dates, LANES), jnp.bfloat16),
    ]
    if halo is not None:
        operands.append(halo)
        specs.append(pl.BlockSpec(memory_space=pl.ANY))
        scratch += [pltpu.VMEM(halo.shape, halo.dtype), pltpu.SemaphoreType.DMA]
    outs = pl.pallas_call(
        functools.partial(
            pack_kernel, ends, first, blocks, col_groups, segments, halo is not None
        ),
        grid=(1,),
        out_shape=shapes * peers,
        in_specs=specs,
        out_specs=[pl.BlockSpec(memory_space=pltpu.VMEM)] * (peers * chunks),
        scratch_shapes=scratch,
        compiler_params=pltpu.CompilerParams(vmem_limit_bytes=36 << 20),
        cost_estimate=pl.CostEstimate(
            flops=10**8, bytes_accessed=blocks * 3 * 10**6, transcendentals=0
        ),
        name="pack",
    )(*operands)
    return [list(outs[chunk::chunks]) for chunk in range(chunks)]


def patch_kernel(tiles, col_groups, segments, *refs):
    halo_ref, refs = refs[0], refs[1:]
    peers = (len(refs) - 4) // 2
    outs, (halo, planes, held, sems) = refs[peers:-4], refs[-4:]
    sent, parts, dates, _ = held.shape
    me = lax.axis_index("date")
    fetch = pltpu.make_async_copy(halo_ref, halo, sems.at[0])
    fetch.start()
    shape = (parts * dates // 16, 16, LANES)

    def keep_edge(block, j, part, plane):
        planes[block, j, part] = plane

    def piece(block, j):
        return planes[block, j]

    for offset, out in enumerate(outs):
        target = me ^ offset

        @pl.when(lax.rem(target, col_groups) == 0)
        def _(out=out, target=target):
            read = pltpu.make_async_copy(out, held, sems.at[1])
            read.start()
            if offset < col_groups:
                fetch.wait()
                edge_planes(halo, keep_edge)
            read.wait()
            masks = {}
            if segments == 1:
                for tile in range(tiles):
                    total = held[tile].reshape(shape)
                    total = compose(total, tile, range(LEFT), piece, masks)
                    held[tile] = total.reshape(held.shape[1:])
            else:
                segment = target // col_groups

                def one_tile(index, carry):
                    tile, last = segment * tiles + index - 1, segments * tiles - 1
                    total = held[index].reshape(shape)
                    total = compose_at(total, tile, last, range(LEFT), piece)
                    held[index] = total.reshape(held.shape[1:])
                    return carry

                lax.fori_loop(0, sent, one_tile, 0)
            write = pltpu.make_async_copy(held, out, sems.at[2])
            write.start()
            write.wait()


def patch(blocks, halo, tiles, col_groups, segments):
    peers = len(blocks)
    _, parts, dates, _ = blocks[0].shape
    anywhere = pl.BlockSpec(memory_space=pl.ANY)
    return pl.pallas_call(
        functools.partial(patch_kernel, tiles, col_groups, segments),
        out_shape=[jax.ShapeDtypeStruct(block.shape, block.dtype) for block in blocks],
        in_specs=[anywhere] * (1 + peers),
        out_specs=[anywhere] * peers,
        scratch_shapes=[
            pltpu.VMEM(halo.shape, halo.dtype),
            pltpu.VMEM((halo.shape[3] // LANES, LEFT, parts, dates, LANES), jnp.bfloat16),
            pltpu.VMEM(blocks[0].shape, jnp.bfloat16),
            pltpu.SemaphoreType.DMA((3,)),
        ],
        input_output_aliases={1 + m: m for m in range(peers)},
        compiler_params=pltpu.CompilerParams(vmem_limit_bytes=16 << 20),
        name="patch",
    )(halo, *blocks)


def slot_rows(first):
    lane = lax.broadcasted_iota(jnp.int32, (16, LANES), 1)
    place = (lane - first) & (LANES - 1)
    column = (place * 57) >> 10
    return place - TILE_ROWS * column, column < BOX_COLS


def as_mask(inside):
    return jnp.where(inside, 1.0, 0.0).astype(jnp.bfloat16)[None]


def window_pair(real, imag, k, e, row_now, row_next):
    shape = (-1, 16, LANES)
    begin, spill = STEP_ROWS * e, STEP_ROWS * e + BOX_ROWS - TILE_ROWS
    now, after = row_now >= begin, row_next < spill + STEP_ROWS
    both, a, b = [], real[k].reshape(shape), imag[k].reshape(shape)
    a, b = a * as_mask(now), b * as_mask(now)
    if spill > 0:
        first = as_mask(now | (row_next < spill))
        second = as_mask((row_now >= begin + STEP_ROWS) | after)
        a = a + real[k + 1].reshape(shape) * as_mask(after)
        b = b + imag[k + 1].reshape(shape) * as_mask(after)
    else:
        first = as_mask(now & (row_now < BOX_ROWS))
        second = as_mask(row_now >= STEP_ROWS)
    for window in (first, second):
        parts = [(part * window).reshape(real.shape[1:]) for part in (a, b)]
        both.append(jnp.concatenate(parts, axis=1))
    return a.reshape(real.shape[1:]), b.reshape(real.shape[1:]), both


def coherence_pair(a, b, both, diagonal, held, place):
    count = a.shape[0]
    left = jnp.concatenate(
        [jnp.concatenate([a, b], axis=1), jnp.concatenate([b, -a], axis=1)], axis=0
    )
    sums = lax.dot_general(
        left, jnp.concatenate(both, axis=0), CONTRACT_LAST, preferred_element_type=jnp.float32
    )
    for index in range(2):
        real = sums[:count, index * count : (index + 1) * count]
        imag = sums[count:, index * count : (index + 1) * count]
        energy = jnp.sum(jnp.where(diagonal, real, 0.0), axis=0, keepdims=True) * (1 / NBOX)
        factor = lax.rsqrt(energy + POWER_EPS)
        down = jnp.sum(jnp.where(diagonal, factor, 0.0), axis=1, keepdims=True)
        weights = down * (factor * (1 / NBOX))
        held[place + index, :count] = (real * weights).astype(jnp.bfloat16)
        held[place + index, count:] = (imag * weights).astype(jnp.bfloat16)


def iterate(held, pixels, dates):
    row = lax.broadcasted_iota(jnp.int32, (8, dates), 0)
    odd = (row & 1) == 1
    sign = jnp.where((row & 2) == 2, -1.0, 1.0)
    start = jnp.concatenate([jnp.where(odd, 0.0, sign), jnp.where(odd, -sign, 0.0)], axis=1)
    vectors = [start.astype(jnp.bfloat16)] * pixels
    for sweep in range(ITERS):
        scaled = []
        for place in range(pixels):
            product = jnp.dot(vectors[place], held[place], preferred_element_type=jnp.float32)
            square = product * product
            square = square + pltpu.roll(square, 1, 0)
            total = jnp.sum(square, axis=1, keepdims=True) * (1 / dates) + POWER_EPS
            scaled.append(product * lax.rsqrt(total))
        if sweep + 1 < ITERS:
            vectors = [
                jnp.concatenate([v, pltpu.roll(v, 7, 0)], axis=1).astype(jnp.bfloat16)
                for v in scaled
            ]
    return scaled


def batch_of(pixels):
    return max(size for size in range(SLOTS, BATCH + 1, SLOTS) if pixels % size == 0)


def link_kernel(peers, carried, earlier, start, padded, last, *refs):
    sources, refs = refs[:peers], refs[peers:]
    before, refs = refs[: peers * carried], refs[peers * carried :]
    done, refs = refs[:earlier], refs[earlier:]
    outs, (real, imag, held, linked, sems) = refs[:-5], refs[-5:]
    sent, _, dates, _ = sources[0].shape
    all_dates = peers * dates
    base = 0 if padded else 2 if carried else 1
    copies = []

    def fetch(tiles, part, at, peer):
        room = (real, imag)[part].at[pl.ds(at, tiles.shape[0]), pl.ds(peer * dates, dates)]
        copies.append(pltpu.make_async_copy(tiles.at[:, part], room, sems.at[len(copies)]))
        copies[-1].start()

    for peer, source in enumerate(sources):
        for part in range(2):
            fetch(source, part, base, peer)
            if carried:
                tiles = before[peer]
                fetch(tiles.at[pl.ds(tiles.shape[0] - 2, 2)], part, 0, peer)
    zero = jnp.zeros((all_dates, LANES), jnp.bfloat16)
    for tiles in (real, imag):
        if not carried and not padded:
            tiles[0] = zero
        if last and not padded:
            tiles[base + sent] = zero
    for copy in copies:
        copy.wait()
    pixels = linked.shape[1]
    batch = batch_of(pixels)
    diagonal = lax.broadcasted_iota(
        jnp.int32, (all_dates, all_dates), 0
    ) == lax.broadcasted_iota(jnp.int32, (all_dates, all_dates), 1)

    def step(index, carry):
        rows_of = {}

        def rows_at(k):
            if k not in rows_of:
                tile = start // SLOTS - 1 + index * (batch // SLOTS) + k
                if padded:
                    tile = tile + lax.axis_index("date") // padded * (sent - 2)
                row, used = slot_rows(tile * TILE_ROWS)
                rows_of[k] = jnp.where(used, row, -1), jnp.where(used, row, LANES)
            return rows_of[k]

        for place in range(0, batch, 2):
            k, e = divmod(place + SLOTS - LEAD, SLOTS)
            at = index * (batch // SLOTS) + k
            a, b, both = window_pair(real, imag, at, e, rows_at(k)[0], rows_at(k + 1)[1])
            coherence_pair(a, b, both, diagonal, held, place)
        for place, tile in enumerate(iterate(held, batch, all_dates)):
            for part in range(2):
                linked[part, pl.ds(index * batch + place, 1)] = tile[part : part + 1]
        return carry

    lax.fori_loop(0, pixels // batch, step, 0)
    for part in range(2):
        vectors = linked[part]
        if not last:
            outs[0][part] = vectors
            continue
        vectors = jnp.concatenate([ref[part] for ref in done] + [vectors], axis=0)
        flat = jnp.transpose(vectors)
        for peer, out in enumerate(outs):
            out[part] = flat[peer * dates : (peer + 1) * dates]


def link(sources, before, done, start, pixels, padded, last):
    peers = len(sources)
    sent, parts, dates, _ = sources[0].shape
    all_dates = peers * dates
    whole = pl.BlockSpec(memory_space=pltpu.VMEM)
    operands = list(sources) + list(before)
    specs = [pl.BlockSpec(memory_space=pl.ANY)] * len(operands)
    operands += done
    specs += [whole] * len(done)
    if last:
        rows = start + pixels
        outs = [jax.ShapeDtypeStruct((parts, dates, rows), jnp.float32)] * peers
    else:
        outs = [jax.ShapeDtypeStruct((parts, pixels, all_dates), jnp.float32)]
    kept = sent + 3
    kernel = functools.partial(
        link_kernel, peers, len(before) > 0, len(done), start, padded, last
    )
    return pl.pallas_call(
        kernel,
        grid=(1,),
        out_shape=outs,
        in_specs=specs,
        out_specs=[whole] * len(outs),
        scratch_shapes=[
            pltpu.VMEM((kept, all_dates, LANES), jnp.bfloat16),
            pltpu.VMEM((kept, all_dates, LANES), jnp.bfloat16),
            pltpu.VMEM((batch_of(pixels), 2 * all_dates, all_dates), jnp.bfloat16),
            pltpu.VMEM((2, pixels, all_dates), jnp.float32),
            pltpu.SemaphoreType.DMA((4 * peers,)),
        ],
        compiler_params=pltpu.CompilerParams(vmem_limit_bytes=20 << 20),
        cost_estimate=pl.CostEstimate(
            flops=pixels * 30 * 10**6, bytes_accessed=10**6, transcendentals=0
        ),
        name="link",
    )(*operands)


def swap(blocks, axis):
    count = len(blocks)
    return [blocks[0]] + [
        lax.ppermute(blocks[m], axis, [(i, i ^ m) for i in range(count)]) for m in range(1, count)
    ]


def place_kernel(peers, out_cols, *refs):
    blocks, out = refs[:peers], refs[peers]
    rows = blocks[0].shape[2]
    me = lax.axis_index("date")
    for target in range(peers):
        value = blocks[target][...]
        for other in range(1, peers):
            value = jnp.where(me == other, blocks[target ^ other][...], value)
        segment = target // out_cols * rows
        out[:, :, target % out_cols, segment : segment + rows] = value


def place_blocks(blocks, out_cols, segments):
    parts, dates, rows = blocks[0].shape
    whole = pl.BlockSpec(memory_space=pltpu.VMEM)
    return pl.pallas_call(
        functools.partial(place_kernel, len(blocks), out_cols),
        out_shape=jax.ShapeDtypeStruct((parts, dates, out_cols, rows * segments), jnp.float32),
        in_specs=[whole] * len(blocks),
        out_specs=whole,
        compiler_params=pltpu.CompilerParams(vmem_limit_bytes=8 << 20),
        name="place",
    )(*blocks)


def chunk_ends(tiles, segments):
    if segments > 1 or tiles < 8:
        return [tiles]
    return [tiles * FIRST // 32, tiles]


def on_device(acquisitions, valid_dates):
    peers = lax.axis_size("date")
    strips = lax.axis_size("space")
    parts, dates, cols, rows = acquisitions.shape
    out_cols = cols // STEP_COLS
    segments = peers // out_cols
    tiles = rows // TILE_ROWS // segments
    pixels = rows // STEP_ROWS // segments
    ends = chunk_ends(tiles, segments)
    first, *rest = ends
    ranges = [blocks_of(0, first, rows, segments)]
    if rest:
        ranges.append(blocks_of(first, tiles, rows, segments))
    halos = [
        lax.ppermute(edges, "space", [(i, i + 1) for i in range(strips - 1)])
        for edges in edge(acquisitions, valid_dates, ranges)
    ]
    (blocks,) = pack(acquisitions, valid_dates, None, peers, [0, first], out_cols, segments)
    outgoing = [patch(blocks, halos[0], first, out_cols, segments)]
    if rest:
        outgoing += pack(acquisitions, valid_dates, halos[1], peers, ends, out_cols, segments)
    incoming = [swap(blocks, "date") for blocks in outgoing]
    done, start = [], 0
    for index, blocks in enumerate(incoming):
        last = index == len(ends) - 1
        stop = pixels if last else (ends[index] - 1) * SLOTS
        before = incoming[index - 1] if index else []
        result = link(
            blocks, before, done if last else [], start, stop - start,
            0 if segments == 1 else out_cols, last,
        )
        done, start = done + list(result), stop
    incoming = swap(result, "date")
    return place_blocks(incoming, out_cols, segments)


def solution(mesh):
    in_specs = (P(None, "date", "space", None), P("date", "space", None))
    out_specs = P(None, "date", "space", None)
    return jax.shard_map(
        on_device, mesh=mesh, in_specs=in_specs, out_specs=out_specs, check_vma=False
    )
```

```python
import functools

import jax
import jax.numpy as jnp
from jax import lax
from jax.experimental import pallas as pl
from jax.experimental.pallas import tpu as pltpu
from jax.sharding import PartitionSpec as P

BOX_ROWS = 15
BOX_COLS = 7
STEP_ROWS = 3
STEP_COLS = 6
ITERS = 4
MARGIN = 6
NBOX = 105
POWER_EPS = 1e-05

LANES = 128
TILE_ROWS = 18
SLOTS = TILE_ROWS // STEP_ROWS
LEAD = MARGIN // STEP_ROWS
LEFT = STEP_COLS // 2
BATCH = 60
FIRST = 19
CONTRACT_LAST = (((1,), (1,)), ((), ()))


def lane_mask(first, count):
    lane = lax.broadcasted_iota(jnp.int32, (16, LANES), 1)
    inside = ((lane - first) & (LANES - 1)) < count
    return (jnp.where(inside, 1.0, 0.0).astype(jnp.bfloat16) > 0)[None]


def choose(mask, yes, no):
    return jnp.where(jnp.broadcast_to(mask, yes.shape), yes, no)


def edge_kernel(first, ranges, *refs):
    acq_ref, valid_ref, *outs, planes = refs
    parts, dates, _, rows = acq_ref.shape
    stride = planes.shape[2] // dates
    span = slice(first // 8 * 8, first // 8 * 8 + 8)
    offset = first % 8

    def one_date(date, carry):
        keep = valid_ref[date, span].astype(jnp.float32)
        for part in range(parts):
            value = acq_ref[part, date, span].astype(jnp.float32) * keep
            for block in range(planes.shape[1]):
                width = min(LANES, rows - block * LANES)
                planes[part, block, pl.ds(date * stride, 8), :width] = value[
                    :, block * LANES : block * LANES + width
                ]
        return carry

    for part in range(parts):
        planes[part, planes.shape[1] - 1] = jnp.zeros(planes.shape[2:], jnp.float32)
    lax.fori_loop(0, dates, one_date, 0, unroll=4)
    for j in range(LEFT):
        for part in range(parts):
            for out, span in zip(outs, ranges):
                for index, block in enumerate(span):
                    plane = planes[part, block, pl.ds(offset + j, dates, stride=stride), :]
                    lanes = slice(index * LANES, (index + 1) * LANES)
                    out[j, part, :, lanes] = plane.astype(out.dtype)


def edge(acquisitions, valid_dates, ranges):
    parts, dates, cols, rows = acquisitions.shape
    blocks = -(-rows // LANES)
    at = (cols - LEFT) // 16
    shapes = [
        jax.ShapeDtypeStruct((LEFT, parts, dates, len(span) * LANES), acquisitions.dtype)
        for span in ranges
    ]
    return pl.pallas_call(
        functools.partial(edge_kernel, cols - LEFT - at * 16, ranges),
        grid=(1,),
        out_shape=shapes,
        in_specs=[
            pl.BlockSpec((parts, dates, 16, rows), lambda i: (0, 0, at, 0)),
            pl.BlockSpec((dates, 16, rows), lambda i: (0, at, 0)),
        ],
        out_specs=[pl.BlockSpec(shape.shape, lambda i: (0, 0, 0, 0)) for shape in shapes],
        scratch_shapes=[pltpu.VMEM((parts, blocks, dates * 9, LANES), jnp.float32)],
        compiler_params=pltpu.CompilerParams(vmem_limit_bytes=60 << 20),
        name="edge",
    )(acquisitions, valid_dates)


def turn(plane, j):
    return pltpu.roll(plane, TILE_ROWS * j, 1) if j else plane


def edge_planes(halo, keep):
    for block in range(halo.shape[3] // LANES):
        at = block * LANES
        for j in range(LEFT):
            for part in range(halo.shape[1]):
                plane = halo[j, part, :, at : at + LANES].astype(jnp.float32)
                keep(block, j, part, turn(plane, j).astype(jnp.bfloat16))


def compose(total, tile, columns, piece, masks):
    for j in columns:
        row, end = tile * TILE_ROWS, (tile + 1) * TILE_ROWS
        while row < end:
            block = row // LANES
            stop = min(end, (block + 1) * LANES)
            key = ((row + TILE_ROWS * j) % LANES, stop - row)
            if key not in masks:
                masks[key] = lane_mask(*key)
            total = choose(masks[key], piece(block, j).reshape(total.shape), total)
            row = stop
    return total


def compose_at(total, tile, last, columns, piece):
    kept = jnp.where((tile >= 0) & (tile <= last), TILE_ROWS, 0)
    row = jnp.clip(tile, 0, last) * TILE_ROWS
    low, high = row // LANES, (row + TILE_ROWS - 1) // LANES
    split = jnp.where(high == low, TILE_ROWS, high * LANES - row)
    for j in columns:
        start = row + TILE_ROWS * j
        for block, first, count in (
            (low, start, jnp.minimum(split, kept)),
            (high, start + split, jnp.minimum(TILE_ROWS - split, kept)),
        ):
            total = choose(lane_mask(first, count), piece(block, j).reshape(total.shape), total)
    return total


def pack_kernel(ends, first_block, blocks, col_groups, segments, *refs):
    acq_refs, refs = refs[:blocks], refs[blocks:]
    valid_refs, refs = refs[:blocks], refs[blocks:]
    outs, (planes, shifted) = refs[:-2], refs[-2:]
    parts, dates, cols, _ = acq_refs[0].shape
    stride = planes.shape[2] // dates
    me = lax.axis_index("date")

    def one_date(date, carry):
        for block in range(blocks):
            keep = valid_refs[block][date].astype(jnp.float32)
            for part in range(parts):
                value = acq_refs[block][part, date].astype(jnp.float32) * keep
                planes[part, block, pl.ds(date * stride, cols)] = value
        return carry

    lax.fori_loop(0, dates, one_date, 0, unroll=4)

    def one_block(block, carry):
        for group in range(col_groups):
            for j in range(BOX_COLS):
                column = group * STEP_COLS - LEFT + j
                for part in range(parts):
                    if column >= 0:
                        plane = planes[part, block, pl.ds(column, dates, stride=stride), :]
                        shifted[group, block, j, part] = turn(plane, j).astype(jnp.bfloat16)
        return carry

    lax.fori_loop(0, blocks, one_block, 0)

    zero = jnp.zeros((parts, dates, LANES), jnp.bfloat16)
    for block in range(blocks):
        for j in range(LEFT):
            shifted[0, block, j] = zero
    masks = {}
    chunks = len(ends) - 1
    empty = jnp.zeros((parts * dates // 16, 16, LANES), jnp.bfloat16)
    for offset in range(len(outs) // chunks):
        mine = outs[offset * chunks : (offset + 1) * chunks]
        target = me ^ offset
        group = lax.rem(target, col_groups)

        def piece(block, j):
            return shifted[group, block - first_block, j]

        if segments == 1:
            for tile in range(ends[0], ends[-1]):
                chunk = sum(tile >= end for end in ends[1:])
                total = compose(empty, tile, range(BOX_COLS), piece, masks)
                mine[chunk][tile - ends[chunk]] = total.reshape(parts, dates, LANES)
        else:
            tiles, segment = ends[-1], target // col_groups

            def one_tile(index, carry):
                tile, last = segment * tiles + index - 1, segments * tiles - 1
                total = compose_at(empty, tile, last, range(BOX_COLS), piece)
                mine[0][index] = total.reshape(parts, dates, LANES)
                return carry

            lax.fori_loop(0, tiles + 2, one_tile, 0)


def blocks_of(low, high, rows, segments):
    if segments > 1:
        return range(-(-rows // LANES))
    return range(low * TILE_ROWS // LANES, -(-high * TILE_ROWS // LANES))


def pack(acquisitions, valid_dates, peers, ends, col_groups, segments):
    parts, dates, cols, rows = acquisitions.shape
    span = blocks_of(ends[0], ends[-1], rows, segments)
    first, blocks = span[0], len(span)
    sent = [high - low + (2 if segments > 1 else 0) for low, high in zip(ends, ends[1:])]

    def block_specs(shape):
        return [
            pl.BlockSpec(
                shape + (LANES,), functools.partial(lambda b, i: (0,) * len(shape) + (b,), first + k)
            )
            for k in range(blocks)
        ]

    chunks = len(sent)
    shapes = [jax.ShapeDtypeStruct((n, parts, dates, LANES), jnp.bfloat16) for n in sent]
    operands = [acquisitions] * blocks + [valid_dates] * blocks
    specs = block_specs((parts, dates, cols)) + block_specs((dates, cols))
    scratch = [
        pltpu.VMEM((parts, blocks, dates * (cols + 1), LANES), jnp.float32),
        pltpu.VMEM((col_groups, blocks, BOX_COLS, parts, dates, LANES), jnp.bfloat16),
    ]
    outs = pl.pallas_call(
        functools.partial(pack_kernel, ends, first, blocks, col_groups, segments),
        grid=(1,),
        out_shape=shapes * peers,
        in_specs=specs,
        out_specs=[pl.BlockSpec(memory_space=pltpu.VMEM)] * (peers * chunks),
        scratch_shapes=scratch,
        compiler_params=pltpu.CompilerParams(vmem_limit_bytes=36 << 20),
        cost_estimate=pl.CostEstimate(
            flops=10**8, bytes_accessed=blocks * 3 * 10**6, transcendentals=0
        ),
        name="pack",
    )(*operands)
    return [list(outs[chunk::chunks]) for chunk in range(chunks)]


def patch_kernel(low, high, first_block, col_groups, segments, *refs):
    halo_ref, refs = refs[0], refs[1:]
    peers = (len(refs) - 4) // 2
    outs, (halo, planes, held, sems) = refs[peers:-4], refs[-4:]
    sent, parts, dates, _ = held.shape
    me = lax.axis_index("date")
    fetch = pltpu.make_async_copy(halo_ref, halo, sems.at[0])
    fetch.start()
    shape = (parts * dates // 16, 16, LANES)

    def keep_edge(block, j, part, plane):
        planes[block, j, part] = plane

    def piece(block, j):
        return planes[block - first_block, j]

    for offset, out in enumerate(outs):
        target = me ^ offset

        @pl.when(lax.rem(target, col_groups) == 0)
        def _(out=out, target=target):
            read = pltpu.make_async_copy(out, held, sems.at[1])
            read.start()
            if offset < col_groups:
                fetch.wait()
                edge_planes(halo, keep_edge)
            read.wait()
            masks = {}
            if segments == 1:
                for tile in range(low, high):
                    total = held[tile - low].reshape(shape)
                    total = compose(total, tile, range(LEFT), piece, masks)
                    held[tile - low] = total.reshape(held.shape[1:])
            else:
                tiles, segment = high, target // col_groups

                def one_tile(index, carry):
                    tile, last = segment * tiles + index - 1, segments * tiles - 1
                    total = held[index].reshape(shape)
                    total = compose_at(total, tile, last, range(LEFT), piece)
                    held[index] = total.reshape(held.shape[1:])
                    return carry

                lax.fori_loop(0, sent, one_tile, 0)
            write = pltpu.make_async_copy(held, out, sems.at[2])
            write.start()
            write.wait()


def patch(blocks, halo, low, high, first_block, col_groups, segments):
    peers = len(blocks)
    _, parts, dates, _ = blocks[0].shape
    anywhere = pl.BlockSpec(memory_space=pl.ANY)
    return pl.pallas_call(
        functools.partial(patch_kernel, low, high, first_block, col_groups, segments),
        out_shape=[jax.ShapeDtypeStruct(block.shape, block.dtype) for block in blocks],
        in_specs=[anywhere] * (1 + peers),
        out_specs=[anywhere] * peers,
        scratch_shapes=[
            pltpu.VMEM(halo.shape, halo.dtype),
            pltpu.VMEM((halo.shape[3] // LANES, LEFT, parts, dates, LANES), jnp.bfloat16),
            pltpu.VMEM(blocks[0].shape, jnp.bfloat16),
            pltpu.SemaphoreType.DMA((3,)),
        ],
        input_output_aliases={1 + m: m for m in range(peers)},
        compiler_params=pltpu.CompilerParams(vmem_limit_bytes=16 << 20),
        name="patch",
    )(halo, *blocks)


def slot_rows(first):
    lane = lax.broadcasted_iota(jnp.int32, (16, LANES), 1)
    place = (lane - first) & (LANES - 1)
    column = (place * 57) >> 10
    return place - TILE_ROWS * column, column < BOX_COLS


def as_mask(inside):
    return jnp.where(inside, 1.0, 0.0).astype(jnp.bfloat16)[None]


def window_pair(real, imag, k, e, row_now, row_next):
    shape = (-1, 16, LANES)
    begin, spill = STEP_ROWS * e, STEP_ROWS * e + BOX_ROWS - TILE_ROWS
    now, after = row_now >= begin, row_next < spill + STEP_ROWS
    both, a, b = [], real[k].reshape(shape), imag[k].reshape(shape)
    a, b = a * as_mask(now), b * as_mask(now)
    if spill > 0:
        first = as_mask(now | (row_next < spill))
        second = as_mask((row_now >= begin + STEP_ROWS) | after)
        a = a + real[k + 1].reshape(shape) * as_mask(after)
        b = b + imag[k + 1].reshape(shape) * as_mask(after)
    else:
        first = as_mask(now & (row_now < BOX_ROWS))
        second = as_mask(row_now >= STEP_ROWS)
    for window in (first, second):
        parts = [(part * window).reshape(real.shape[1:]) for part in (a, b)]
        both.append(jnp.concatenate(parts, axis=1))
    return a.reshape(real.shape[1:]), b.reshape(real.shape[1:]), both


def stack_parts(real, imag):
    row = lax.broadcasted_iota(jnp.int32, real.shape, 0)
    both = jnp.where((row & 1) == 1, imag, real)
    return jnp.where((row & 2) == 2, -both, both)


def column_sums(matrix):
    total = jnp.sum(matrix.astype(jnp.float32).reshape(-1, 8, matrix.shape[1]), axis=0)
    for distance in (4, 2, 1):
        total = total + pltpu.roll(total, distance, 0)
    return total


def coherence_pair(a, b, both, diagonal, held, place):
    matrices, begun = held
    count = a.shape[0]
    left = jnp.concatenate(
        [jnp.concatenate([a, b], axis=1), jnp.concatenate([b, -a], axis=1)], axis=0
    )
    sums = lax.dot_general(
        left, jnp.concatenate(both, axis=0), CONTRACT_LAST, preferred_element_type=jnp.float32
    )
    for index in range(2):
        real = sums[:count, index * count : (index + 1) * count]
        imag = sums[count:, index * count : (index + 1) * count]
        energy = jnp.sum(jnp.where(diagonal, real, 0.0), axis=0, keepdims=True) * (1 / NBOX)
        factor = lax.rsqrt(energy + POWER_EPS)
        down = jnp.sum(jnp.where(diagonal, factor, 0.0), axis=1, keepdims=True)
        weights = down * (factor * (1 / NBOX))
        real, imag = (real * weights).astype(jnp.bfloat16), (imag * weights).astype(jnp.bfloat16)
        matrices[place + index, :count] = real
        matrices[place + index, count:] = imag
        begun[place + index] = stack_parts(column_sums(real), -column_sums(imag))


def iterate(held, pixels, dates):
    matrices, begun = held
    products = [begun[place] for place in range(pixels)]
    for sweep in range(ITERS):
        if sweep:
            products = [
                jnp.dot(vectors[place], matrices[place], preferred_element_type=jnp.float32)
                for place in range(pixels)
            ]
        scaled = []
        for product in products:
            square = product * product
            square = square + pltpu.roll(square, 1, 0)
            total = jnp.sum(square, axis=1, keepdims=True) * (1 / dates) + POWER_EPS
            scaled.append(product * lax.rsqrt(total))
        vectors = [
            jnp.concatenate([v, pltpu.roll(v, 7, 0)], axis=1).astype(jnp.bfloat16) for v in scaled
        ]
    return scaled


def batch_of(pixels):
    return max(size for size in range(SLOTS, BATCH + 1, SLOTS) if pixels % size == 0)


def link_kernel(peers, carried, earlier, start, padded, last, *refs):
    sources, refs = refs[:peers], refs[peers:]
    before, refs = refs[: peers * carried], refs[peers * carried :]
    done, refs = refs[:earlier], refs[earlier:]
    outs, (real, imag, *held, linked, sems) = refs[:-8], refs[-8:]
    sent, _, dates, _ = sources[0].shape
    all_dates = peers * dates
    base = 0 if padded else 2 if carried else 1
    copies = []

    def fetch(tiles, part, at, peer):
        room = (real, imag)[part].at[pl.ds(at, tiles.shape[0]), pl.ds(peer * dates, dates)]
        copies.append(pltpu.make_async_copy(tiles.at[:, part], room, sems.at[len(copies)]))
        copies[-1].start()

    for peer, source in enumerate(sources):
        for part in range(2):
            fetch(source, part, base, peer)
            if carried:
                tiles = before[peer]
                fetch(tiles.at[pl.ds(tiles.shape[0] - 2, 2)], part, 0, peer)
    zero = jnp.zeros((all_dates, LANES), jnp.bfloat16)
    for tiles in (real, imag):
        if not carried and not padded:
            tiles[0] = zero
        if last and not padded:
            tiles[base + sent] = zero
    for copy in copies:
        copy.wait()
    pixels = linked.shape[1]
    batch = batch_of(pixels)
    diagonal = lax.broadcasted_iota(
        jnp.int32, (all_dates, all_dates), 0
    ) == lax.broadcasted_iota(jnp.int32, (all_dates, all_dates), 1)

    def gram(index, held):
        rows_of = {}

        def rows_at(k):
            if k not in rows_of:
                tile = start // SLOTS - 1 + index * (batch // SLOTS) + k
                if padded:
                    tile = tile + lax.axis_index("date") // padded * (sent - 2)
                row, used = slot_rows(tile * TILE_ROWS)
                rows_of[k] = jnp.where(used, row, -1), jnp.where(used, row, LANES)
            return rows_of[k]

        for place in range(0, batch, 2):
            k, e = divmod(place + SLOTS - LEAD, SLOTS)
            at = index * (batch // SLOTS) + k
            a, b, both = window_pair(real, imag, at, e, rows_at(k)[0], rows_at(k + 1)[1])
            coherence_pair(a, b, both, diagonal, held, place)

    def power(index, held):
        for place, tile in enumerate(iterate(held, batch, all_dates)):
            for part in range(2):
                linked[part, pl.ds(index * batch + place, 1)] = tile[part : part + 1]

    batches = pixels // batch
    slots = held[:2], held[2:]
    gram(0, slots[0])

    def step(index, carry):
        gram(2 * index + 1, slots[1])
        power(2 * index, slots[0])
        gram(2 * index + 2, slots[0])
        power(2 * index + 1, slots[1])
        return carry

    lax.fori_loop(0, (batches - 1) // 2, step, 0)
    if batches % 2 == 0:
        gram(batches - 1, slots[1])
        power(batches - 2, slots[0])
    power(batches - 1, slots[(batches - 1) % 2])
    for part in range(2):
        vectors = linked[part]
        if not last:
            outs[0][part] = vectors
            continue
        vectors = jnp.concatenate([ref[part] for ref in done] + [vectors], axis=0)
        flat = jnp.transpose(vectors)
        for peer, out in enumerate(outs):
            out[part] = flat[peer * dates : (peer + 1) * dates]


def link(sources, before, done, start, pixels, padded, last):
    peers = len(sources)
    sent, parts, dates, _ = sources[0].shape
    all_dates = peers * dates
    whole = pl.BlockSpec(memory_space=pltpu.VMEM)
    operands = list(sources) + list(before)
    specs = [pl.BlockSpec(memory_space=pl.ANY)] * len(operands)
    operands += done
    specs += [whole] * len(done)
    if last:
        rows = start + pixels
        outs = [jax.ShapeDtypeStruct((parts, dates, rows), jnp.float32)] * peers
    else:
        outs = [jax.ShapeDtypeStruct((parts, pixels, all_dates), jnp.float32)]
    kept = sent + 3
    kernel = functools.partial(
        link_kernel, peers, len(before) > 0, len(done), start, padded, last
    )
    return pl.pallas_call(
        kernel,
        grid=(1,),
        out_shape=outs,
        in_specs=specs,
        out_specs=[whole] * len(outs),
        scratch_shapes=[
            pltpu.VMEM((kept, all_dates, LANES), jnp.bfloat16),
            pltpu.VMEM((kept, all_dates, LANES), jnp.bfloat16),
            *[
                pltpu.VMEM((batch_of(pixels), 2 * all_dates, all_dates), jnp.bfloat16),
                pltpu.VMEM((batch_of(pixels), 8, all_dates), jnp.float32),
            ]
            * 2,
            pltpu.VMEM((2, pixels, all_dates), jnp.float32),
            pltpu.SemaphoreType.DMA((4 * peers,)),
        ],
        compiler_params=pltpu.CompilerParams(vmem_limit_bytes=(17 << 20) + kept * (128 << 10)),
        cost_estimate=pl.CostEstimate(
            flops=pixels * 30 * 10**6, bytes_accessed=10**6, transcendentals=0
        ),
        name="link",
    )(*operands)


def swap(blocks, axis):
    count = len(blocks)
    return [blocks[0]] + [
        lax.ppermute(blocks[m], axis, [(i, i ^ m) for i in range(count)]) for m in range(1, count)
    ]


def place_kernel(peers, out_cols, *refs):
    blocks, out = refs[:peers], refs[peers]
    rows = blocks[0].shape[2]
    me = lax.axis_index("date")
    for target in range(peers):
        value = blocks[target][...]
        for other in range(1, peers):
            value = jnp.where(me == other, blocks[target ^ other][...], value)
        segment = target // out_cols * rows
        out[:, :, target % out_cols, segment : segment + rows] = value


def place_blocks(blocks, out_cols, segments):
    parts, dates, rows = blocks[0].shape
    whole = pl.BlockSpec(memory_space=pltpu.VMEM)
    return pl.pallas_call(
        functools.partial(place_kernel, len(blocks), out_cols),
        out_shape=jax.ShapeDtypeStruct((parts, dates, out_cols, rows * segments), jnp.float32),
        in_specs=[whole] * len(blocks),
        out_specs=whole,
        compiler_params=pltpu.CompilerParams(vmem_limit_bytes=8 << 20),
        name="place",
    )(*blocks)


def chunk_ends(tiles, segments):
    if segments > 1 or tiles < 8:
        return [tiles]
    return [tiles * FIRST // 32, tiles]


def on_device(acquisitions, valid_dates):
    peers = lax.axis_size("date")
    strips = lax.axis_size("space")
    parts, dates, cols, rows = acquisitions.shape
    out_cols = cols // STEP_COLS
    segments = peers // out_cols
    tiles = rows // TILE_ROWS // segments
    pixels = rows // STEP_ROWS // segments
    ends = chunk_ends(tiles, segments)
    first, *rest = ends
    ranges = [blocks_of(0, first, rows, segments)]
    if rest:
        ranges.append(blocks_of(first, tiles, rows, segments))
    halos = [
        lax.ppermute(edges, "space", [(i, i + 1) for i in range(strips - 1)])
        for edges in edge(acquisitions, valid_dates, ranges)
    ]
    outgoing = []
    for low, high, span, halo in zip([0] + ends, ends, ranges, halos):
        (blocks,) = pack(acquisitions, valid_dates, peers, [low, high], out_cols, segments)
        outgoing.append(patch(blocks, halo, low, high, span[0], out_cols, segments))
    incoming = [swap(blocks, "date") for blocks in outgoing]
    done, start = [], 0
    for index, blocks in enumerate(incoming):
        last = index == len(ends) - 1
        stop = pixels if last else (ends[index] - 1) * SLOTS
        before = incoming[index - 1] if index else []
        result = link(
            blocks, before, done if last else [], start, stop - start,
            0 if segments == 1 else out_cols, last,
        )
        done, start = done + list(result), stop
    incoming = swap(result, "date")
    return place_blocks(incoming, out_cols, segments)


def solution(mesh):
    in_specs = (P(None, "date", "space", None), P("date", "space", None))
    out_specs = P(None, "date", "space", None)
    return jax.shard_map(
        on_device, mesh=mesh, in_specs=in_specs, out_specs=out_specs, check_vma=False
    )
```

```python
import functools

import jax
import jax.numpy as jnp
from jax import lax
from jax.experimental import pallas as pl
from jax.experimental.pallas import tpu as pltpu
from jax.sharding import PartitionSpec as P

BOX_ROWS = 15
BOX_COLS = 7
STEP_ROWS = 3
STEP_COLS = 6
ITERS = 4
MARGIN = 6
NBOX = 105
POWER_EPS = 1e-05

LANES = 128
TILE_ROWS = 18
SLOTS = TILE_ROWS // STEP_ROWS
LEAD = MARGIN // STEP_ROWS
LEFT = STEP_COLS // 2
BATCH = 60
FIRST = 19
CONTRACT_LAST = (((1,), (1,)), ((), ()))


def lane_mask(first, count):
    lane = lax.broadcasted_iota(jnp.int32, (16, LANES), 1)
    inside = ((lane - first) & (LANES - 1)) < count
    return (jnp.where(inside, 1.0, 0.0).astype(jnp.bfloat16) > 0)[None]


def choose(mask, yes, no):
    return jnp.where(jnp.broadcast_to(mask, yes.shape), yes, no)


def edge_kernel(first, ranges, *refs):
    acq_ref, valid_ref, *outs, planes = refs
    parts, dates, _, rows = acq_ref.shape
    stride = planes.shape[2] // dates
    span = slice(first // 8 * 8, first // 8 * 8 + 8)
    offset = first % 8

    def one_date(date, carry):
        keep = valid_ref[date, span].astype(jnp.float32)
        for part in range(parts):
            value = acq_ref[part, date, span].astype(jnp.float32) * keep
            for block in range(planes.shape[1]):
                width = min(LANES, rows - block * LANES)
                planes[part, block, pl.ds(date * stride, 8), :width] = value[
                    :, block * LANES : block * LANES + width
                ]
        return carry

    for part in range(parts):
        planes[part, planes.shape[1] - 1] = jnp.zeros(planes.shape[2:], jnp.float32)
    lax.fori_loop(0, dates, one_date, 0, unroll=4)
    for j in range(LEFT):
        for part in range(parts):
            for out, span in zip(outs, ranges):
                for index, block in enumerate(span):
                    plane = planes[part, block, pl.ds(offset + j, dates, stride=stride), :]
                    lanes = slice(index * LANES, (index + 1) * LANES)
                    out[j, part, :, lanes] = plane.astype(out.dtype)


def edge(acquisitions, valid_dates, ranges):
    parts, dates, cols, rows = acquisitions.shape
    blocks = -(-rows // LANES)
    at = (cols - LEFT) // 16
    shapes = [
        jax.ShapeDtypeStruct((LEFT, parts, dates, len(span) * LANES), acquisitions.dtype)
        for span in ranges
    ]
    return pl.pallas_call(
        functools.partial(edge_kernel, cols - LEFT - at * 16, ranges),
        grid=(1,),
        out_shape=shapes,
        in_specs=[
            pl.BlockSpec((parts, dates, 16, rows), lambda i: (0, 0, at, 0)),
            pl.BlockSpec((dates, 16, rows), lambda i: (0, at, 0)),
        ],
        out_specs=[pl.BlockSpec(shape.shape, lambda i: (0, 0, 0, 0)) for shape in shapes],
        scratch_shapes=[pltpu.VMEM((parts, blocks, dates * 9, LANES), jnp.float32)],
        compiler_params=pltpu.CompilerParams(vmem_limit_bytes=60 << 20),
        name="edge",
    )(acquisitions, valid_dates)


def turn(plane, j):
    return pltpu.roll(plane, TILE_ROWS * j, 1) if j else plane


def edge_planes(halo, keep):
    for block in range(halo.shape[3] // LANES):
        at = block * LANES
        for j in range(LEFT):
            for part in range(halo.shape[1]):
                plane = halo[j, part, :, at : at + LANES].astype(jnp.float32)
                keep(block, j, part, turn(plane, j).astype(jnp.bfloat16))


def compose(total, tile, columns, piece, masks):
    for j in columns:
        row, end = tile * TILE_ROWS, (tile + 1) * TILE_ROWS
        while row < end:
            block = row // LANES
            stop = min(end, (block + 1) * LANES)
            key = ((row + TILE_ROWS * j) % LANES, stop - row)
            if key not in masks:
                masks[key] = lane_mask(*key)
            total = choose(masks[key], piece(block, j).reshape(total.shape), total)
            row = stop
    return total


def compose_at(total, tile, last, columns, piece):
    kept = jnp.where((tile >= 0) & (tile <= last), TILE_ROWS, 0)
    row = jnp.clip(tile, 0, last) * TILE_ROWS
    low, high = row // LANES, (row + TILE_ROWS - 1) // LANES
    split = jnp.where(high == low, TILE_ROWS, high * LANES - row)
    for j in columns:
        start = row + TILE_ROWS * j
        for block, first, count in (
            (low, start, jnp.minimum(split, kept)),
            (high, start + split, jnp.minimum(TILE_ROWS - split, kept)),
        ):
            total = choose(lane_mask(first, count), piece(block, j).reshape(total.shape), total)
    return total


def pack_kernel(ends, first_block, blocks, col_groups, segments, *refs):
    acq_refs, refs = refs[:blocks], refs[blocks:]
    valid_refs, refs = refs[:blocks], refs[blocks:]
    outs, (planes, shifted) = refs[:-2], refs[-2:]
    parts, dates, cols, _ = acq_refs[0].shape
    stride = planes.shape[2] // dates
    me = lax.axis_index("date")

    def one_date(date, carry):
        for block in range(blocks):
            keep = valid_refs[block][date].astype(jnp.float32)
            for part in range(parts):
                value = acq_refs[block][part, date].astype(jnp.float32) * keep
                planes[part, block, pl.ds(date * stride, cols)] = value
        return carry

    lax.fori_loop(0, dates, one_date, 0, unroll=4)

    def one_block(block, carry):
        for group in range(col_groups):
            for j in range(BOX_COLS):
                column = group * STEP_COLS - LEFT + j
                for part in range(parts):
                    if column >= 0:
                        plane = planes[part, block, pl.ds(column, dates, stride=stride), :]
                        shifted[group, block, j, part] = turn(plane, j).astype(jnp.bfloat16)
        return carry

    lax.fori_loop(0, blocks, one_block, 0)

    zero = jnp.zeros((parts, dates, LANES), jnp.bfloat16)
    for block in range(blocks):
        for j in range(LEFT):
            shifted[0, block, j] = zero
    masks = {}
    chunks = len(ends) - 1
    empty = jnp.zeros((parts * dates // 16, 16, LANES), jnp.bfloat16)
    for offset in range(len(outs) // chunks):
        mine = outs[offset * chunks : (offset + 1) * chunks]
        target = me ^ offset
        group = lax.rem(target, col_groups)

        def piece(block, j):
            return shifted[group, block - first_block, j]

        if segments == 1:
            for tile in range(ends[0], ends[-1]):
                chunk = sum(tile >= end for end in ends[1:])
                total = compose(empty, tile, range(BOX_COLS), piece, masks)
                mine[chunk][tile - ends[chunk]] = total.reshape(parts, dates, LANES)
        else:
            tiles, segment = ends[-1], target // col_groups

            def one_tile(index, carry):
                tile, last = segment * tiles + index - 1, segments * tiles - 1
                total = compose_at(empty, tile, last, range(BOX_COLS), piece)
                mine[0][index] = total.reshape(parts, dates, LANES)
                return carry

            lax.fori_loop(0, tiles + 2, one_tile, 0)


def blocks_of(low, high, rows, segments):
    if segments > 1:
        return range(-(-rows // LANES))
    return range(low * TILE_ROWS // LANES, -(-high * TILE_ROWS // LANES))


def pack(acquisitions, valid_dates, peers, ends, col_groups, segments):
    parts, dates, cols, rows = acquisitions.shape
    span = blocks_of(ends[0], ends[-1], rows, segments)
    first, blocks = span[0], len(span)
    sent = [high - low + (2 if segments > 1 else 0) for low, high in zip(ends, ends[1:])]

    def block_specs(shape):
        return [
            pl.BlockSpec(
                shape + (LANES,), functools.partial(lambda b, i: (0,) * len(shape) + (b,), first + k)
            )
            for k in range(blocks)
        ]

    chunks = len(sent)
    shapes = [jax.ShapeDtypeStruct((n, parts, dates, LANES), jnp.bfloat16) for n in sent]
    operands = [acquisitions] * blocks + [valid_dates] * blocks
    specs = block_specs((parts, dates, cols)) + block_specs((dates, cols))
    scratch = [
        pltpu.VMEM((parts, blocks, dates * (cols + 1), LANES), jnp.float32),
        pltpu.VMEM((col_groups, blocks, BOX_COLS, parts, dates, LANES), jnp.bfloat16),
    ]
    outs = pl.pallas_call(
        functools.partial(pack_kernel, ends, first, blocks, col_groups, segments),
        grid=(1,),
        out_shape=shapes * peers,
        in_specs=specs,
        out_specs=[pl.BlockSpec(memory_space=pltpu.VMEM)] * (peers * chunks),
        scratch_shapes=scratch,
        compiler_params=pltpu.CompilerParams(vmem_limit_bytes=36 << 20),
        cost_estimate=pl.CostEstimate(
            flops=10**8, bytes_accessed=blocks * 3 * 10**6, transcendentals=0
        ),
        name="pack",
    )(*operands)
    return [list(outs[chunk::chunks]) for chunk in range(chunks)]


def patch_kernel(low, high, first_block, col_groups, segments, *refs):
    halo_ref, refs = refs[0], refs[1:]
    peers = (len(refs) - 4) // 2
    outs, (halo, planes, held, sems) = refs[peers:-4], refs[-4:]
    sent, parts, dates, _ = held.shape
    me = lax.axis_index("date")
    fetch = pltpu.make_async_copy(halo_ref, halo, sems.at[0])
    fetch.start()
    shape = (parts * dates // 16, 16, LANES)

    def keep_edge(block, j, part, plane):
        planes[block, j, part] = plane

    def piece(block, j):
        return planes[block - first_block, j]

    for offset, out in enumerate(outs):
        target = me ^ offset

        @pl.when(lax.rem(target, col_groups) == 0)
        def _(out=out, target=target):
            read = pltpu.make_async_copy(out, held, sems.at[1])
            read.start()
            if offset < col_groups:
                fetch.wait()
                edge_planes(halo, keep_edge)
            read.wait()
            masks = {}
            if segments == 1:
                for tile in range(low, high):
                    total = held[tile - low].reshape(shape)
                    total = compose(total, tile, range(LEFT), piece, masks)
                    held[tile - low] = total.reshape(held.shape[1:])
            else:
                tiles, segment = high, target // col_groups

                def one_tile(index, carry):
                    tile, last = segment * tiles + index - 1, segments * tiles - 1
                    total = held[index].reshape(shape)
                    total = compose_at(total, tile, last, range(LEFT), piece)
                    held[index] = total.reshape(held.shape[1:])
                    return carry

                lax.fori_loop(0, sent, one_tile, 0)
            write = pltpu.make_async_copy(held, out, sems.at[2])
            write.start()
            write.wait()


def patch(blocks, halo, low, high, first_block, col_groups, segments):
    peers = len(blocks)
    _, parts, dates, _ = blocks[0].shape
    anywhere = pl.BlockSpec(memory_space=pl.ANY)
    return pl.pallas_call(
        functools.partial(patch_kernel, low, high, first_block, col_groups, segments),
        out_shape=[jax.ShapeDtypeStruct(block.shape, block.dtype) for block in blocks],
        in_specs=[anywhere] * (1 + peers),
        out_specs=[anywhere] * peers,
        scratch_shapes=[
            pltpu.VMEM(halo.shape, halo.dtype),
            pltpu.VMEM((halo.shape[3] // LANES, LEFT, parts, dates, LANES), jnp.bfloat16),
            pltpu.VMEM(blocks[0].shape, jnp.bfloat16),
            pltpu.SemaphoreType.DMA((3,)),
        ],
        input_output_aliases={1 + m: m for m in range(peers)},
        compiler_params=pltpu.CompilerParams(vmem_limit_bytes=16 << 20),
        name="patch",
    )(halo, *blocks)


def slot_rows(first):
    lane = lax.broadcasted_iota(jnp.int32, (16, LANES), 1)
    place = (lane - first) & (LANES - 1)
    column = (place * 57) >> 10
    return place - TILE_ROWS * column, column < BOX_COLS


def as_mask(inside):
    return jnp.where(inside, 1.0, 0.0).astype(jnp.bfloat16)[None]


def window_pair(real, imag, k, e, row_now, row_next):
    shape = (-1, 16, LANES)
    begin, spill = STEP_ROWS * e, STEP_ROWS * e + BOX_ROWS - TILE_ROWS
    now, after = row_now >= begin, row_next < spill + STEP_ROWS
    both, a, b = [], real[k].reshape(shape), imag[k].reshape(shape)
    a, b = a * as_mask(now), b * as_mask(now)
    if spill > 0:
        first = as_mask(now | (row_next < spill))
        second = as_mask((row_now >= begin + STEP_ROWS) | after)
        a = a + real[k + 1].reshape(shape) * as_mask(after)
        b = b + imag[k + 1].reshape(shape) * as_mask(after)
    else:
        first = as_mask(now & (row_now < BOX_ROWS))
        second = as_mask(row_now >= STEP_ROWS)
    for window in (first, second):
        parts = [(part * window).reshape(real.shape[1:]) for part in (a, b)]
        both.append(jnp.concatenate(parts, axis=1))
    return a.reshape(real.shape[1:]), b.reshape(real.shape[1:]), both


def stack_parts(real, imag):
    row = lax.broadcasted_iota(jnp.int32, real.shape, 0)
    both = jnp.where((row & 1) == 1, imag, real)
    return jnp.where((row & 2) == 2, -both, both)


def column_sums(matrix):
    total = jnp.sum(matrix.astype(jnp.float32).reshape(-1, 8, matrix.shape[1]), axis=0)
    for distance in (4, 2, 1):
        total = total + pltpu.roll(total, distance, 0)
    return total


def coherence_pair(a, b, both, diagonal, held, place):
    matrices, begun = held
    count = a.shape[0]
    left = jnp.concatenate(
        [jnp.concatenate([a, b], axis=1), jnp.concatenate([b, -a], axis=1)], axis=0
    )
    sums = lax.dot_general(
        left, jnp.concatenate(both, axis=0), CONTRACT_LAST, preferred_element_type=jnp.float32
    )
    for index in range(2):
        real = sums[:count, index * count : (index + 1) * count]
        imag = sums[count:, index * count : (index + 1) * count]
        energy = jnp.sum(jnp.where(diagonal, real, 0.0), axis=0, keepdims=True) * (1 / NBOX)
        factor = lax.rsqrt(energy + POWER_EPS)
        down = jnp.sum(jnp.where(diagonal, factor, 0.0), axis=1, keepdims=True)
        weights = down * (factor * (1 / NBOX))
        real, imag = (real * weights).astype(jnp.bfloat16), (imag * weights).astype(jnp.bfloat16)
        matrices[place + index, :count] = real
        matrices[place + index, count:] = imag
        begun[place + index] = stack_parts(column_sums(real), -column_sums(imag))


def iterate(held, pixels, dates):
    matrices, begun = held
    products = [begun[place] for place in range(pixels)]
    for sweep in range(ITERS):
        if sweep:
            products = [
                jnp.dot(vectors[place], matrices[place], preferred_element_type=jnp.float32)
                for place in range(pixels)
            ]
        scaled = []
        for product in products:
            square = product * product
            square = square + pltpu.roll(square, 1, 0)
            total = jnp.sum(square, axis=1, keepdims=True) * (1 / dates) + POWER_EPS
            scaled.append(product * lax.rsqrt(total))
        vectors = [
            jnp.concatenate([v, pltpu.roll(v, 7, 0)], axis=1).astype(jnp.bfloat16) for v in scaled
        ]
    return scaled


def batch_of(pixels):
    return max(size for size in range(SLOTS, BATCH + 1, SLOTS) if pixels % size == 0)


def link_kernel(peers, carried, earlier, start, padded, last, *refs):
    sources, refs = refs[:peers], refs[peers:]
    before, refs = refs[: peers * carried], refs[peers * carried :]
    done, refs = refs[:earlier], refs[earlier:]
    outs, (real, imag, *held, linked, sems) = refs[:-8], refs[-8:]
    sent, _, dates, _ = sources[0].shape
    all_dates = peers * dates
    base = 0 if padded else 2 if carried else 1
    copies = []

    def fetch(tiles, part, at, peer):
        room = (real, imag)[part].at[pl.ds(at, tiles.shape[0]), pl.ds(peer * dates, dates)]
        copies.append(pltpu.make_async_copy(tiles.at[:, part], room, sems.at[len(copies)]))
        copies[-1].start()

    for peer, source in enumerate(sources):
        for part in range(2):
            fetch(source, part, base, peer)
            if carried:
                tiles = before[peer]
                fetch(tiles.at[pl.ds(tiles.shape[0] - 2, 2)], part, 0, peer)
    zero = jnp.zeros((all_dates, LANES), jnp.bfloat16)
    for tiles in (real, imag):
        if not carried and not padded:
            tiles[0] = zero
        if last and not padded:
            tiles[base + sent] = zero
    for copy in copies:
        copy.wait()
    pixels = linked.shape[1]
    batch = batch_of(pixels)
    diagonal = lax.broadcasted_iota(
        jnp.int32, (all_dates, all_dates), 0
    ) == lax.broadcasted_iota(jnp.int32, (all_dates, all_dates), 1)

    def gram(index, held):
        rows_of = {}

        def rows_at(k):
            if k not in rows_of:
                tile = start // SLOTS - 1 + index * (batch // SLOTS) + k
                if padded:
                    tile = tile + lax.axis_index("date") // padded * (sent - 2)
                row, used = slot_rows(tile * TILE_ROWS)
                rows_of[k] = jnp.where(used, row, -1), jnp.where(used, row, LANES)
            return rows_of[k]

        for place in range(0, batch, 2):
            k, e = divmod(place + SLOTS - LEAD, SLOTS)
            at = index * (batch // SLOTS) + k
            a, b, both = window_pair(real, imag, at, e, rows_at(k)[0], rows_at(k + 1)[1])
            coherence_pair(a, b, both, diagonal, held, place)

    def power(index, held):
        for place, tile in enumerate(iterate(held, batch, all_dates)):
            for part in range(2):
                linked[part, pl.ds(index * batch + place, 1)] = tile[part : part + 1]

    batches = pixels // batch
    slots = held[:2], held[2:]
    gram(0, slots[0])

    def step(index, carry):
        gram(2 * index + 1, slots[1])
        power(2 * index, slots[0])
        gram(2 * index + 2, slots[0])
        power(2 * index + 1, slots[1])
        return carry

    lax.fori_loop(0, (batches - 1) // 2, step, 0)
    if batches % 2 == 0:
        gram(batches - 1, slots[1])
        power(batches - 2, slots[0])
    power(batches - 1, slots[(batches - 1) % 2])
    for part in range(2):
        vectors = linked[part]
        if not last:
            outs[0][part] = vectors
            continue
        vectors = jnp.concatenate([ref[part] for ref in done] + [vectors], axis=0)
        flat = jnp.transpose(vectors)
        for peer, out in enumerate(outs):
            out[part] = flat[peer * dates : (peer + 1) * dates].astype(out.dtype)


def link(sources, before, done, start, pixels, padded, last):
    peers = len(sources)
    sent, parts, dates, _ = sources[0].shape
    all_dates = peers * dates
    whole = pl.BlockSpec(memory_space=pltpu.VMEM)
    operands = list(sources) + list(before)
    specs = [pl.BlockSpec(memory_space=pl.ANY)] * len(operands)
    operands += done
    specs += [whole] * len(done)
    if last:
        rows = start + pixels
        away = jax.ShapeDtypeStruct((parts, dates, rows), jnp.bfloat16)
        outs = [jax.ShapeDtypeStruct((parts, dates, rows), jnp.float32)] + [away] * (peers - 1)
    else:
        outs = [jax.ShapeDtypeStruct((parts, pixels, all_dates), jnp.float32)]
    kept = sent + 3
    kernel = functools.partial(
        link_kernel, peers, len(before) > 0, len(done), start, padded, last
    )
    return pl.pallas_call(
        kernel,
        grid=(1,),
        out_shape=outs,
        in_specs=specs,
        out_specs=[whole] * len(outs),
        scratch_shapes=[
            pltpu.VMEM((kept, all_dates, LANES), jnp.bfloat16),
            pltpu.VMEM((kept, all_dates, LANES), jnp.bfloat16),
            *[
                pltpu.VMEM((batch_of(pixels), 2 * all_dates, all_dates), jnp.bfloat16),
                pltpu.VMEM((batch_of(pixels), 8, all_dates), jnp.float32),
            ]
            * 2,
            pltpu.VMEM((2, pixels, all_dates), jnp.float32),
            pltpu.SemaphoreType.DMA((4 * peers,)),
        ],
        compiler_params=pltpu.CompilerParams(vmem_limit_bytes=(17 << 20) + kept * (128 << 10)),
        cost_estimate=pl.CostEstimate(
            flops=pixels * 30 * 10**6, bytes_accessed=10**6, transcendentals=0
        ),
        name="link",
    )(*operands)


def swap(blocks, axis):
    count = len(blocks)
    return [blocks[0]] + [
        lax.ppermute(blocks[m], axis, [(i, i ^ m) for i in range(count)]) for m in range(1, count)
    ]


def place_kernel(peers, out_cols, *refs):
    blocks, out = refs[:peers], refs[peers]
    rows = blocks[0].shape[2]
    me = lax.axis_index("date")
    for target in range(peers):
        value = blocks[target][...].astype(jnp.float32)
        for other in range(1, peers):
            value = jnp.where(
                me == other, blocks[target ^ other][...].astype(jnp.float32), value
            )
        segment = target // out_cols * rows
        out[:, :, target % out_cols, segment : segment + rows] = value


def place_blocks(blocks, out_cols, segments):
    parts, dates, rows = blocks[0].shape
    whole = pl.BlockSpec(memory_space=pltpu.VMEM)
    return pl.pallas_call(
        functools.partial(place_kernel, len(blocks), out_cols),
        out_shape=jax.ShapeDtypeStruct((parts, dates, out_cols, rows * segments), jnp.float32),
        in_specs=[whole] * len(blocks),
        out_specs=whole,
        compiler_params=pltpu.CompilerParams(vmem_limit_bytes=8 << 20),
        name="place",
    )(*blocks)


def chunk_ends(tiles, segments):
    if segments > 1 or tiles < 8:
        return [tiles]
    return [tiles * FIRST // 32, tiles]


def on_device(acquisitions, valid_dates):
    peers = lax.axis_size("date")
    strips = lax.axis_size("space")
    parts, dates, cols, rows = acquisitions.shape
    out_cols = cols // STEP_COLS
    segments = peers // out_cols
    tiles = rows // TILE_ROWS // segments
    pixels = rows // STEP_ROWS // segments
    ends = chunk_ends(tiles, segments)
    first, *rest = ends
    ranges = [blocks_of(0, first, rows, segments)]
    if rest:
        ranges.append(blocks_of(first, tiles, rows, segments))
    halos = [
        lax.ppermute(edges, "space", [(i, i + 1) for i in range(strips - 1)])
        for edges in edge(acquisitions, valid_dates, ranges)
    ]
    outgoing = []
    for low, high, span, halo in zip([0] + ends, ends, ranges, halos):
        (blocks,) = pack(acquisitions, valid_dates, peers, [low, high], out_cols, segments)
        outgoing.append(patch(blocks, halo, low, high, span[0], out_cols, segments))
    incoming = [swap(blocks, "date") for blocks in outgoing]
    done, start = [], 0
    for index, blocks in enumerate(incoming):
        last = index == len(ends) - 1
        stop = pixels if last else (ends[index] - 1) * SLOTS
        before = incoming[index - 1] if index else []
        result = link(
            blocks, before, done if last else [], start, stop - start,
            0 if segments == 1 else out_cols, last,
        )
        done, start = done + list(result), stop
    incoming = swap(result, "date")
    return place_blocks(incoming, out_cols, segments)


def solution(mesh):
    in_specs = (P(None, "date", "space", None), P("date", "space", None))
    out_specs = P(None, "date", "space", None)
    return jax.shard_map(
        on_device, mesh=mesh, in_specs=in_specs, out_specs=out_specs, check_vma=False
    )
```
